256 devices in a mesh: dp: 32 (over z_hi, x, core), token: 8 (over z_lo, y).
Axes of the slice: x: 4, y: 4, z: 8 (z_hi: 4, z_lo: 2; z = z_hi * 2 + z_lo), core: 2. Of those that a mesh axis runs over, the one named last changes fastest.
Arguments:
- block_input: bfloat16 [8192, 8, 1536], P('dp', 'token'), may hold values from -6 to 6
- out_cotangent: bfloat16 [8192, 8, 1536], P('dp', 'token'), may hold values from -6 to 6
- w_in: bfloat16 [8, 1536, 2, 1024], P('token'), may hold values from -0.15625 to 0.15625
- w_out: bfloat16 [8, 1536, 1024], P('token'), may hold values from -0.1875 to 0.1875
Outputs:
- input_grad: bfloat16 [8192, 8, 1536], P('dp', 'token')
- w_in_grad: bfloat16 [8, 1536, 2, 1024], P('token', 'dp')
- w_out_grad: bfloat16 [8, 1536, 1024], P('token', 'dp')
The draws below stay inside these ranges and needn't reach their ends.
All inputs are finite; a program needn't handle non-finite values.
Results may differ from the reference program's by a relative error of at most 0.022.
Values may be sent and summed in bfloat16 or wider, within the bound.
No kernel may reach another device: no remote copies, remote signals or barrier semaphores. Data moves between devices by JAX's collectives and lax.ppermute only.
A program may use at most 128 MiB of HBM per device.

```python
import jax
import jax.numpy as jnp
from jax import lax

D = 1536
FF = 1024
SAMP_DEV = 256
TOKENS = 8
BATCH = 8192
N_DP = 32


def with_spikes(entries, rng, source, target, parts, factor):
    owner, partner = [(jnp.arange(entries.shape[position]) // (entries.shape[position] // parts)).reshape([-1 if axis == position else 1 for axis in range(entries.ndim)]) for position in (source, target)]
    chosen = jax.random.permutation(rng, parts)[partner]
    strong = (owner == chosen) | (owner == (partner + parts // 2) % parts)
    return jnp.where(strong, factor * entries, entries)


def block_scale(rng, dims, split, smallest, top_value):
    level = 1.0
    for axis_at, shards_of in split:
        heights = jax.random.uniform(jax.random.fold_in(jax.random.fold_in(rng, 6), axis_at), (shards_of,), jnp.float32, smallest / len(split), top_value / len(split))
        level = level * jnp.repeat(jnp.exp(heights), dims[axis_at] // shards_of).reshape((-1,) + (1,) * (len(dims) - 1 - axis_at))
    return level


def bell_draw(key, shape, scale, most, cuts=(), held_as=jnp.bfloat16):
    drawn = scale * jax.random.normal(key, shape, jnp.float32)
    if cuts:
        drawn = drawn * block_scale(key, shape, cuts, -0.22, 0.18)
    return jnp.clip(drawn, -most, most).astype(held_as)


def gaussian_with(rng, shape, spread, reach, split, heavy, held_as=jnp.bfloat16):
    drawn = spread * jax.random.normal(rng, shape, jnp.float32)
    if split:
        drawn = drawn * block_scale(rng, shape, split, -0.22, 0.18)
    return jnp.clip(with_spikes(drawn, jax.random.fold_in(rng, 3), *heavy), -reach, reach).astype(held_as)


def setup_inputs(seed: int = 0) -> dict:
    key_of = jax.random.split(jax.random.key(seed), 5)
    return {
        "block_input": gaussian_with(key_of[0], (BATCH, TOKENS, D), 1.0, 6.0, ((0, 32), (1, 8)), (0, 2, 32, 2.75)),
        "out_cotangent": gaussian_with(key_of[1], (BATCH, TOKENS, D), 1.0, 6.0, ((0, 32), (1, 8)), (0, 2, 32, 2.75)),
        "w_in": bell_draw(key_of[2], (TOKENS, D, 2, FF), D ** -0.5, 0.15625, ((0, 8),)),
        "w_out": bell_draw(key_of[3], (TOKENS, D, FF), FF ** -0.5, 0.1875, ((0, 8),)),
    }


eps = 1e-06

def contract(left, right, dims_left, dims_right):
    return lax.dot_general(left, right, ((dims_left, dims_right), ((), ())), preferred_element_type=jnp.float32)

def normalize(values):
    scale = lax.rsqrt(lax.optimization_barrier(jnp.mean(values * values, axis=-1, keepdims=True)) + eps)
    return (values * scale, scale)

def norm_back(normed, scale, grads):
    return scale * (grads - normed * lax.optimization_barrier(jnp.mean(grads * normed, axis=-1, keepdims=True)))

def rounded(values):
    return lax.optimization_barrier(values.astype(jnp.bfloat16)).astype(jnp.float32)

def per_token(operands):
    pre_norm, cotangent, weight_in, weight_out = operands
    batch, width = pre_norm.shape
    hidden_units = weight_out.shape[1]
    normed, scale_one = normalize(pre_norm)
    state = normed.astype(jnp.bfloat16)
    flat_in = weight_in.reshape(width, 2 * hidden_units)
    both = contract(state, flat_in, (1,), (0,)).reshape(batch, 2, hidden_units)
    gate = both[:, 0]
    up_part = both[:, 1]
    sigma = jax.nn.sigmoid(gate)
    silu_gate = gate * sigma
    hidden = (silu_gate * up_part).astype(jnp.bfloat16)
    ffn_sum = contract(hidden, weight_out, (1,), (1,)) + state.astype(jnp.float32)
    out_normed, scale_two = normalize(ffn_sum)
    out_grad = norm_back(out_normed, scale_two, cotangent.astype(jnp.float32))
    out_grad16 = out_grad.astype(jnp.bfloat16)
    hidden_grad = contract(out_grad16, weight_out, (1,), (0,))
    gate_grad = hidden_grad * up_part * sigma * (1.0 + gate * (1.0 - sigma))
    up_grad = hidden_grad * silu_gate
    inner_grad = jnp.stack([gate_grad, up_grad], axis=1).astype(jnp.bfloat16).reshape(batch, 2 * hidden_units)
    state_grad = contract(inner_grad, flat_in, (1,), (1,)) + out_grad
    pre_grad = norm_back(normed, scale_one, state_grad)
    groups = (state.reshape(N_DP, SAMP_DEV, width), inner_grad.reshape(N_DP, SAMP_DEV, 2 * hidden_units), out_grad16.reshape(N_DP, SAMP_DEV, width), hidden.reshape(N_DP, SAMP_DEV, hidden_units))

    def add_group(carry, group):
        state_g, inner_g, outg_g, hidden_g = group
        part_in = rounded(contract(state_g, inner_g, (0,), (0,)))
        part_out = rounded(contract(outg_g, hidden_g, (0,), (0,)))
        return ((carry[0] + part_in, carry[1] + part_out), None)
    start = (jnp.zeros((width, 2 * hidden_units), jnp.float32), jnp.zeros((width, hidden_units), jnp.float32))
    totals, unused = lax.scan(add_group, start, groups)
    in_grad = totals[0].reshape(width, 2, hidden_units).astype(jnp.bfloat16)
    return (pre_grad, in_grad, totals[1].astype(jnp.bfloat16))

def reference(block_input, out_cotangent, w_in, w_out):
    batch, count, width = block_input.shape
    head = width // count
    mixed = block_input.reshape(batch, count, count, head).transpose(0, 2, 1, 3).reshape(batch, count, width)
    pre_norm = block_input.astype(jnp.float32) + mixed.astype(jnp.float32)
    pre_grad, in_grad, out_grad = lax.map(per_token, (pre_norm.transpose(1, 0, 2), out_cotangent.transpose(1, 0, 2), w_in, w_out))
    pre_grad = pre_grad.transpose(1, 0, 2)
    returned = pre_grad.reshape(batch, count, count, head).transpose(0, 2, 1, 3).reshape(batch, count, width)
    input_grad = (pre_grad + returned).astype(jnp.bfloat16)
    return (input_grad, in_grad, out_grad)
```

```python
import functools

import jax
import jax.numpy as jnp
from jax import lax
from jax.experimental import pallas as pl
from jax.experimental.pallas import tpu as pltpu
from jax.sharding import PartitionSpec as P

EPS = 1e-06
TOK = 8
F32 = jnp.float32
BF16 = jnp.bfloat16
VMEM_LIMIT = 56 * 1024 * 1024


def low_lanes(rows):
    return lax.broadcasted_iota(jnp.int32, (rows, 128), 1) < 64


def turn(values):
    return pltpu.roll(values, 64, 1)


def pack(read, packed_ref):
    samples = packed_ref.shape[1] * 2 // 3
    half = samples // 2
    low, low_half = low_lanes(samples), low_lanes(half)
    for pair in range(TOK // 2):
        first, middle, last = read(3 * pair), read(3 * pair + 1), read(3 * pair + 2)
        even, odd = packed_ref.at[2 * pair], packed_ref.at[2 * pair + 1]
        even[:samples] = first.astype(BF16)
        even[samples:] = jnp.where(low_half, middle[:half], turn(middle[half:])).astype(BF16)
        odd[:samples] = turn(jnp.where(low, last, middle)).astype(BF16)
        odd[samples:] = jnp.where(low_half, turn(last[:half]), last[half:]).astype(BF16)


def unpack(packed_ref, write):
    samples = packed_ref.shape[1] * 2 // 3
    low = low_lanes(samples)
    for pair in range(TOK // 2):
        even, odd = packed_ref.at[2 * pair], packed_ref.at[2 * pair + 1]
        turned = turn(odd[:samples].astype(F32))
        rest = even[samples:].astype(F32)
        rest = jnp.concatenate([rest, turn(rest)], axis=0)
        rest_odd = odd[samples:].astype(F32)
        rest_odd = jnp.concatenate([turn(rest_odd), rest_odd], axis=0)
        write(3 * pair, even[:samples].astype(F32))
        write(3 * pair + 1, jnp.where(low, rest, turned))
        write(3 * pair + 2, jnp.where(low, turned, rest_odd))


def tile(t):
    return slice(128 * t, 128 * t + 128)


def pack_kernel(x_ref, packed_ref):
    pack(lambda t: x_ref[:, tile(t)].astype(F32), packed_ref)


def nn(a, b):
    return lax.dot_general(a, b, (((1,), (0,)), ((), ())), preferred_element_type=F32)


def nt(a, b):
    return lax.dot_general(a, b, (((1,), (1,)), ((), ())), preferred_element_type=F32)


def forward_kernel(
    index_ref, x_ref, recv_ref, cot_ref, w_in_hbm, w_out_hbm,
    own_ref, send_ref, normed_ref, scale_ref, grad_ref, grad16_ref, slope_ref, silu_ref,
    w_in, w_out, state, hidden, turned, in_sem, out_sem,
):
    samples, width = x_ref.shape
    ff = w_out.shape[1]
    wide = 256
    steps = ff // wide
    half = width // 2

    def w_in_copy(j, c):
        cols = pl.ds(c * ff + j * wide, wide)
        return pltpu.make_async_copy(w_in_hbm.at[:, cols], w_in.at[:, cols], in_sem.at[2 * j + c])

    for j in range(steps):
        w_in_copy(j, 0).start()
        w_in_copy(j, 1).start()
    out_copy = pltpu.make_async_copy(w_out_hbm, w_out, out_sem)
    out_copy.start()

    rank = index_ref[0]

    def spread(at):
        for b in range(16):
            place = slice(at + 48 * b, at + 48 * b + 48)
            own_ref[place, :] = turned[pl.ds(pl.multiple_of((rank ^ (2 * b)) * 48, 48), 48), :]
            send_ref[place, :] = turned[pl.ds(pl.multiple_of((rank ^ (2 * b + 1)) * 48, 48), 48), :]

    def add_mixed(t, mixed):
        normed_ref[:, tile(t)] = x_ref[:, tile(t)].astype(F32) + mixed

    unpack(recv_ref, add_mixed)
    squares = jnp.zeros((samples, 128), F32)
    for t in range(width // 128):
        v = normed_ref[:, tile(t)]
        squares = squares + v * v
    scale = lax.rsqrt(jnp.sum(squares, axis=1, keepdims=True) / width + EPS)
    scale_ref[...] = jnp.broadcast_to(scale, scale_ref.shape)
    for t in range(width // 128):
        v = normed_ref[:, tile(t)] * scale
        normed_ref[:, tile(t)] = v
        state[:, tile(t)] = v.astype(BF16)

    for j in range(steps):
        cols = slice(wide * j, wide * j + wide)
        w_in_copy(j, 0).wait()
        gate = nn(state[...], w_in[:, cols])
        w_in_copy(j, 1).wait()
        up = nn(state[...], w_in[:, ff + wide * j : ff + wide * j + wide])
        sigma = jax.nn.sigmoid(gate)
        silu_gate = gate * sigma
        part = (silu_gate * up).astype(BF16)
        hidden[:, cols] = part
        send_ref[width + wide * j : width + wide * j + wide, :] = part
        silu_ref[:, cols] = silu_gate
        slope_ref[:, cols] = up * sigma * (1.0 + gate * (1.0 - sigma))

    for t in range(width // 128):
        turned[tile(t), :] = state[:, tile(t)].T
    spread(half)

    out_copy.wait()
    for d in range(width // wide):
        cols = slice(wide * d, wide * d + wide)
        grad_ref[:, cols] = nt(hidden[...], w_out[cols, :]) + state[:, cols].astype(F32)
    squares = jnp.zeros((samples, 128), F32)
    products = jnp.zeros((samples, 128), F32)
    for t in range(width // 128):
        v = grad_ref[:, tile(t)]
        squares = squares + v * v
        products = products + v * cot_ref[:, tile(t)].astype(F32)
    scale_two = lax.rsqrt(jnp.sum(squares, axis=1, keepdims=True) / width + EPS)
    mean = scale_two * jnp.sum(products, axis=1, keepdims=True) / width
    for t in range(width // 128):
        out_normed = grad_ref[:, tile(t)] * scale_two
        g = scale_two * (cot_ref[:, tile(t)].astype(F32) - out_normed * mean)
        grad_ref[:, tile(t)] = g
        g16 = g.astype(BF16)
        grad16_ref[:, tile(t)] = g16
        turned[tile(t), :] = g16.T
    spread(0)


def inner_kernel(grad16_ref, slope_ref, silu_ref, w_out_ref, inner_ref):
    ff = w_out_ref.shape[1]
    wide = 256
    for j in range(ff // wide):
        cols = slice(wide * j, wide * j + wide)
        hidden_grad = nn(grad16_ref[...], w_out_ref[:, cols])
        inner_ref[cols, :] = (hidden_grad * slope_ref[:, cols]).astype(BF16)
        inner_ref[ff + wide * j : ff + wide * j + wide, :] = (hidden_grad * silu_ref[:, cols]).astype(BF16)


def input_kernel(
    inner_ref, w_in_hbm, normed_ref, scale_ref, grad_ref, after_ref, pre_ref, packed_ref, w_in, inner, sem
):
    del after_ref
    samples, width = normed_ref.shape
    wide = 256

    def copy(d):
        rows = pl.ds(d * wide, wide)
        return pltpu.make_async_copy(w_in_hbm.at[rows], w_in.at[rows], sem.at[d])

    for d in range(width // wide):
        copy(d).start()
    for j in range(inner.shape[1] // samples):
        inner[:, samples * j : samples * j + samples] = inner_ref[samples * j : samples * j + samples, :]
    products = jnp.zeros((samples, 128), F32)
    for d in range(width // wide):
        copy(d).wait()
        cols = slice(wide * d, wide * d + wide)
        g = nt(inner[...], w_in[cols, :]) + grad_ref[:, cols]
        pre_ref[:, cols] = g
        p = g * normed_ref[:, cols]
        products = products + p[:, :128] + p[:, 128:]
    mean = jnp.sum(products, axis=1, keepdims=True) / width
    scale = scale_ref[:, :1]
    for t in range(width // 128):
        pre_ref[:, tile(t)] = scale * (pre_ref[:, tile(t)] - normed_ref[:, tile(t)] * mean)
    pack(lambda t: pre_ref[:, tile(t)], packed_ref)


def final_kernel(pre_ref, recv_ref, out_ref):
    def write(t, returned):
        out_ref[:, tile(t)] = (pre_ref[:, tile(t)] + returned).astype(BF16)

    unpack(recv_ref, write)


KEEP_FIRST = ((0, 3, 1, 2), (0, 1, 3, 2))
PARTNERS = ((1, 3), (3, 1))


def grad_kernel(x_first, at, block, own_ref, recv_ref, right_ref, right_recv_ref, after_ref, *outs):
    del after_ref
    rows = own_ref.shape[0] // 2
    wide = 256
    per = outs[0].shape[1] // wide
    for k in range(2 * per):
        flavour, col = divmod(k, per)
        keep, send = outs[2 * flavour], outs[2 * flavour + 1]
        order = KEEP_FIRST[flavour]
        place = slice(block + wide * k, block + wide * k + wide)
        g = nn(own_ref[at : at + rows, :], right_ref[place, :])
        g = (g + nn(recv_ref[at : at + rows, :], right_recv_ref[place, :])).astype(BF16)
        for b in range(16):
            rz, rx = order.index(b // 4), order.index(b % 4)
            to = rx * 4 + rz if x_first else rz * 4 + rx
            target = keep if to < 8 else send
            to = (to % 8) * 48
            target[to : to + 48, wide * col : wide * col + wide] = g[48 * b : 48 * b + 48]


def params():
    return pltpu.CompilerParams(vmem_limit_bytes=VMEM_LIMIT)


VMEM = pl.BlockSpec(memory_space=pltpu.VMEM)
SMEM = pl.BlockSpec(memory_space=pltpu.SMEM)
ANY = pl.BlockSpec(memory_space=pl.ANY)


def cost(flops, moved):
    return pl.CostEstimate(flops=int(flops), bytes_accessed=int(moved), transcendentals=0)


def shape(dims, dtype=BF16):
    return jax.ShapeDtypeStruct(dims, dtype)


def swap(values, distance):
    return lax.ppermute(values, "dp", [(i, i ^ distance) for i in range(32)])


def gradients(x_first, at, block, columns, own, recv, right, right_recv, after, name):
    piece = shape((384, columns // 2))
    moved = (own.size + recv.size + 2 * right.size + 768 * columns) * 2
    return pl.pallas_call(
        functools.partial(grad_kernel, x_first, at, block),
        out_shape=[piece] * 4,
        in_specs=[VMEM] * 4 + [ANY],
        out_specs=[VMEM] * 4,
        compiler_params=params(),
        cost_estimate=cost(2 * 768 * 512 * columns, moved),
        name=name,
    )(own, recv, right, right_recv, after)


def reduce_step(scales, step, keep, send):
    kept, sent = [], []
    for flavour in range(2):
        scale = scales[step // 2]
        got = swap(send[flavour], PARTNERS[flavour][step % 2] * scale)
        total = keep[flavour].astype(F32) + got.astype(F32)
        if step == 3:
            kept.append(total.astype(BF16))
            continue
        half = total.shape[0] // 2
        kept.append(total[:half].astype(BF16))
        sent.append(total[half:].astype(BF16))
    return kept, sent


def local(block_input, out_cotangent, w_in, w_out):
    samples, _, width = block_input.shape
    ff = w_out.shape[2]
    x = block_input[:, 0]
    cotangent = out_cotangent[:, 0]
    flat_in = w_in[0].reshape(width, 2 * ff)
    weight_out = w_out[0]
    packed_shape = shape((TOK, samples * 3 // 2, 128))
    index = lax.axis_index("dp").astype(jnp.int32).reshape(1)

    packed = pl.pallas_call(
        pack_kernel, out_shape=packed_shape, in_specs=[VMEM], out_specs=VMEM, compiler_params=params(),
        cost_estimate=cost(samples * width, 4 * samples * width), name="pack",
    )(x)
    recv = lax.all_to_all(packed, "token", split_axis=0, concat_axis=0, tiled=True)

    full = shape((samples, width), F32)
    gates = shape((samples, ff), F32)
    own, out_send, normed, scale, out_grad, out_grad16, slope, silu = pl.pallas_call(
        forward_kernel,
        out_shape=[
            shape((width, samples)), shape((width + ff, samples)), full, shape((samples, 128), F32), full,
            shape((samples, width)), gates, gates,
        ],
        in_specs=[SMEM, VMEM, VMEM, VMEM, ANY, ANY],
        out_specs=[VMEM] * 8,
        scratch_shapes=[
            pltpu.VMEM((width, 2 * ff), BF16),
            pltpu.VMEM((width, ff), BF16),
            pltpu.VMEM((samples, width), BF16),
            pltpu.VMEM((samples, ff), BF16),
            pltpu.VMEM((width, samples), BF16),
            pltpu.SemaphoreType.DMA((8,)),
            pltpu.SemaphoreType.DMA,
        ],
        compiler_params=params(),
        cost_estimate=cost(6 * samples * width * ff, 18e6),
        name="forward",
    )(index, x, recv, cotangent, flat_in, weight_out)
    out_recv = swap(out_send, 1)

    inner = pl.pallas_call(
        inner_kernel,
        out_shape=shape((2 * ff, samples)),
        in_specs=[VMEM] * 4,
        out_specs=VMEM,
        compiler_params=params(),
        cost_estimate=cost(2 * samples * width * ff, 8e6),
        name="inner",
    )(out_grad16, slope, silu, weight_out)
    inner_recv = swap(inner, 1)

    down = gradients(False, 0, width, ff, own, out_recv, out_send, out_recv, inner, "down_grads")
    up = gradients(True, width // 2, 0, 2 * ff, own, out_recv, inner, inner_recv, down[1], "in_grads")

    pre_grad, back = pl.pallas_call(
        input_kernel,
        out_shape=[full, packed_shape],
        in_specs=[VMEM, ANY, VMEM, VMEM, VMEM, ANY],
        out_specs=[VMEM] * 2,
        scratch_shapes=[
            pltpu.VMEM((width, 2 * ff), BF16),
            pltpu.VMEM((samples, 2 * ff), BF16),
            pltpu.SemaphoreType.DMA((width // 256,)),
        ],
        compiler_params=params(),
        cost_estimate=cost(4 * samples * width * ff, 14e6),
        name="input",
    )(inner, flat_in, normed, scale, out_grad, up[1])
    returned = lax.all_to_all(back, "token", split_axis=0, concat_axis=0, tiled=True)

    down_keep, down_send = down[0::2], down[1::2]
    up_keep, up_send = up[0::2], up[1::2]
    for step in range(4):
        down_keep, down_send = reduce_step((8, 2), step, down_keep, down_send)
        up_keep, up_send = reduce_step((2, 8), step, up_keep, up_send)

    input_grad = pl.pallas_call(
        final_kernel, out_shape=shape((samples, width)), in_specs=[VMEM] * 2, out_specs=VMEM,
        compiler_params=params(), cost_estimate=cost(samples * width, 8 * samples * width), name="final",
    )(pre_grad, returned)
    return (
        input_grad[:, None, :],
        jnp.stack(up_keep, axis=1)[None],
        jnp.concatenate(down_keep, axis=1)[None],
    )


def solution(mesh):
    placed = (
        P("dp", "token", None),
        P("dp", "token", None),
        P("token", None, None, None),
        P("token", None, None),
    )
    return jax.shard_map(
        local,
        mesh=mesh,
        in_specs=placed,
        out_specs=(P("dp", "token", None), P("token", "dp", None, None), P("token", "dp", None)),
        check_vma=False,
    )
```

```python
import functools

import jax
import jax.numpy as jnp
from jax import lax
from jax.experimental import pallas as pl
from jax.experimental.pallas import tpu as pltpu
from jax.sharding import PartitionSpec as P

EPS = 1e-06
TOK = 8
F32 = jnp.float32
BF16 = jnp.bfloat16
VMEM_LIMIT = 56 * 1024 * 1024


def low_lanes(rows):
    return lax.broadcasted_iota(jnp.int32, (rows, 128), 1) < 64


def turn(values):
    return pltpu.roll(values, 64, 1)


def pack(read, packed_ref):
    samples = packed_ref.shape[1] * 2 // 3
    half = samples // 2
    low, low_half = low_lanes(samples), low_lanes(half)
    for pair in range(TOK // 2):
        first, middle, last = read(3 * pair), read(3 * pair + 1), read(3 * pair + 2)
        even, odd = packed_ref.at[2 * pair], packed_ref.at[2 * pair + 1]
        even[:samples] = first.astype(BF16)
        even[samples:] = jnp.where(low_half, middle[:half], turn(middle[half:])).astype(BF16)
        odd[:samples] = turn(jnp.where(low, last, middle)).astype(BF16)
        odd[samples:] = jnp.where(low_half, turn(last[:half]), last[half:]).astype(BF16)


def unpack(packed_ref, write):
    samples = packed_ref.shape[1] * 2 // 3
    low = low_lanes(samples)
    for pair in range(TOK // 2):
        even, odd = packed_ref.at[2 * pair], packed_ref.at[2 * pair + 1]
        turned = turn(odd[:samples].astype(F32))
        rest = even[samples:].astype(F32)
        rest = jnp.concatenate([rest, turn(rest)], axis=0)
        rest_odd = odd[samples:].astype(F32)
        rest_odd = jnp.concatenate([turn(rest_odd), rest_odd], axis=0)
        write(3 * pair, even[:samples].astype(F32))
        write(3 * pair + 1, jnp.where(low, rest, turned))
        write(3 * pair + 2, jnp.where(low, turned, rest_odd))


def tile(t):
    return slice(128 * t, 128 * t + 128)


def pack_kernel(x_ref, packed_ref):
    pack(lambda t: x_ref[:, tile(t)].astype(F32), packed_ref)


def nn(a, b):
    return lax.dot_general(a, b, (((1,), (0,)), ((), ())), preferred_element_type=F32)


def nt(a, b):
    return lax.dot_general(a, b, (((1,), (1,)), ((), ())), preferred_element_type=F32)


def norm_state(x_ref, recv_ref, normed_ref):
    samples, width = x_ref.shape
    sums = [jnp.zeros((samples, 128), F32)]

    def add_mixed(t, mixed):
        v = x_ref[:, tile(t)].astype(F32) + mixed
        normed_ref[:, tile(t)] = v
        sums[0] = sums[0] + v * v

    unpack(recv_ref, add_mixed)
    scale = lax.rsqrt(jnp.sum(sums[0], axis=1, keepdims=True) / width + EPS)
    for t in range(width // 128):
        normed_ref[:, tile(t)] = normed_ref[:, tile(t)] * scale
    return scale


def main_kernel(
    index_ref, x_ref, recv_ref, cot_hbm, w_in_hbm, w_out_hbm,
    own_hbm, send_hbm, inner_hbm, grad16_hbm,
    w_in, w_out, cot, state, grad16, hidden, values, slope, silu, turned, own, send, inner,
    in_sem, out_sem, cot_sem, write_sem,
):
    samples, width = x_ref.shape
    ff = w_out.shape[1]
    wide = 256
    steps = ff // wide
    half = width // 2
    writes = []

    def write(source, target, begin, rows):
        place = pl.ds(begin, rows)
        writes.append(pltpu.make_async_copy(source.at[place], target.at[place], write_sem.at[len(writes)]))
        writes[-1].start()

    def w_in_copy(j, c):
        cols = pl.ds(c * ff + j * wide, wide)
        return pltpu.make_async_copy(w_in_hbm.at[:, cols], w_in.at[:, cols], in_sem.at[2 * j + c])

    for j in range(steps):
        w_in_copy(j, 0).start()
        w_in_copy(j, 1).start()
    out_copy = pltpu.make_async_copy(w_out_hbm, w_out, out_sem)
    out_copy.start()
    cot_copy = pltpu.make_async_copy(cot_hbm, cot, cot_sem)
    cot_copy.start()

    rank = index_ref[0]

    def spread(at):
        for b in range(16):
            place = slice(at + 48 * b, at + 48 * b + 48)
            own[place, :] = turned[pl.ds(pl.multiple_of((rank ^ (2 * b)) * 48, 48), 48), :]
            send[place, :] = turned[pl.ds(pl.multiple_of((rank ^ (2 * b + 1)) * 48, 48), 48), :]
        write(send, send_hbm, at, half)
        write(own, own_hbm, at, half)

    norm_state(x_ref, recv_ref, values)
    for t in range(width // 128):
        state[:, tile(t)] = values[:, tile(t)].astype(BF16)

    for j in range(steps):
        cols = slice(wide * j, wide * j + wide)
        w_in_copy(j, 0).wait()
        gate = nn(state[...], w_in[:, cols])
        w_in_copy(j, 1).wait()
        up = nn(state[...], w_in[:, ff + wide * j : ff + wide * j + wide])
        sigma = jax.nn.sigmoid(gate)
        silu_gate = gate * sigma
        part = (silu_gate * up).astype(BF16)
        hidden[:, cols] = part
        send[width + wide * j : width + wide * j + wide, :] = part
        silu[:, cols] = silu_gate
        slope[:, cols] = up * sigma * (1.0 + gate * (1.0 - sigma))
    write(send, send_hbm, width, ff)

    out_copy.wait()
    for d in range(width // wide):
        cols = slice(wide * d, wide * d + wide)
        values[:, cols] = nt(hidden[...], w_out[cols, :]) + state[:, cols].astype(F32)
    for t in range(width // 128):
        turned[tile(t), :] = state[:, tile(t)].T
    spread(half)
    cot_copy.wait()
    squares = jnp.zeros((samples, 128), F32)
    products = jnp.zeros((samples, 128), F32)
    for t in range(width // 128):
        v = values[:, tile(t)]
        squares = squares + v * v
        products = products + v * cot[:, tile(t)].astype(F32)
    scale = lax.rsqrt(jnp.sum(squares, axis=1, keepdims=True) / width + EPS)
    mean = scale * jnp.sum(products, axis=1, keepdims=True) / width
    for t in range(width // 128):
        out_normed = values[:, tile(t)] * scale
        g16 = (scale * (cot[:, tile(t)].astype(F32) - out_normed * mean)).astype(BF16)
        grad16[:, tile(t)] = g16
        turned[tile(t), :] = g16.T
    write(grad16, grad16_hbm, 0, samples)
    spread(0)
    for j in range(steps):
        cols = slice(wide * j, wide * j + wide)
        hidden_grad = nn(grad16[...], w_out[:, cols])
        inner[cols, :] = (hidden_grad * slope[:, cols]).astype(BF16)
        inner[ff + wide * j : ff + wide * j + wide, :] = (hidden_grad * silu[:, cols]).astype(BF16)
        write(inner, inner_hbm, wide * j, wide)
        write(inner, inner_hbm, ff + wide * j, wide)
    for copy in writes:
        copy.wait()


def input_kernel(
    inner_ref, w_in_hbm, x_ref, recv_ref, grad_ref, after_ref, pre_ref, packed_ref, w_in, inner, normed, sem
):
    del after_ref
    samples, width = x_ref.shape
    wide = 256

    def copy(d):
        rows = pl.ds(d * wide, wide)
        return pltpu.make_async_copy(w_in_hbm.at[rows], w_in.at[rows], sem.at[d])

    for d in range(width // wide):
        copy(d).start()
    scale = norm_state(x_ref, recv_ref, normed)
    for j in range(inner.shape[1] // samples):
        inner[:, samples * j : samples * j + samples] = inner_ref[samples * j : samples * j + samples, :]
    products = jnp.zeros((samples, 128), F32)
    for d in range(width // wide):
        copy(d).wait()
        cols = slice(wide * d, wide * d + wide)
        g = nt(inner[...], w_in[cols, :]) + grad_ref[:, cols].astype(F32)
        pre_ref[:, cols] = g
        p = g * normed[:, cols]
        products = products + p[:, :128] + p[:, 128:]
    mean = jnp.sum(products, axis=1, keepdims=True) / width
    for t in range(width // 128):
        pre_ref[:, tile(t)] = scale * (pre_ref[:, tile(t)] - normed[:, tile(t)] * mean)
    pack(lambda t: pre_ref[:, tile(t)], packed_ref)


def final_kernel(pre_ref, recv_ref, out_ref):
    def write(t, returned):
        out_ref[:, tile(t)] = (pre_ref[:, tile(t)] + returned).astype(BF16)

    unpack(recv_ref, write)


KEEP_FIRST = ((0, 3, 1, 2), (0, 1, 3, 2))
PARTNERS = ((1, 3), (3, 1))


def grad_kernel(x_first, at, block, own_ref, recv_ref, right_ref, right_recv_ref, after_ref, *outs):
    del after_ref
    rows = own_ref.shape[0] // 2
    wide = 256
    per = outs[0].shape[1] // wide
    for k in range(2 * per):
        flavour, col = divmod(k, per)
        keep, send = outs[2 * flavour], outs[2 * flavour + 1]
        order = KEEP_FIRST[flavour]
        place = slice(block + wide * k, block + wide * k + wide)
        g = nn(own_ref[at : at + rows, :], right_ref[place, :])
        g = (g + nn(recv_ref[at : at + rows, :], right_recv_ref[place, :])).astype(BF16)
        for b in range(16):
            rz, rx = order.index(b // 4), order.index(b % 4)
            to = rx * 4 + rz if x_first else rz * 4 + rx
            target = keep if to < 8 else send
            to = (to % 8) * 48
            target[to : to + 48, wide * col : wide * col + wide] = g[48 * b : 48 * b + 48]


def params():
    return pltpu.CompilerParams(vmem_limit_bytes=VMEM_LIMIT)


VMEM = pl.BlockSpec(memory_space=pltpu.VMEM)
SMEM = pl.BlockSpec(memory_space=pltpu.SMEM)
ANY = pl.BlockSpec(memory_space=pl.ANY)


def cost(flops, moved):
    return pl.CostEstimate(flops=int(flops), bytes_accessed=int(moved), transcendentals=0)


def shape(dims, dtype=BF16):
    return jax.ShapeDtypeStruct(dims, dtype)


def swap(values, distance):
    return lax.ppermute(values, "dp", [(i, i ^ distance) for i in range(32)])


def gradients(x_first, at, block, columns, own, recv, right, right_recv, after, name):
    piece = shape((384, columns // 2))
    moved = (own.size + recv.size + 2 * right.size + 768 * columns) * 2
    return pl.pallas_call(
        functools.partial(grad_kernel, x_first, at, block),
        out_shape=[piece] * 4,
        in_specs=[VMEM] * 4 + [ANY],
        out_specs=[VMEM] * 4,
        compiler_params=params(),
        cost_estimate=cost(2 * 768 * 512 * columns, moved),
        name=name,
    )(own, recv, right, right_recv, after)


def reduce_send(scales, step, send):
    return [swap(send[f], PARTNERS[f][step % 2] * scales[step // 2]) for f in range(2)]


def reduce_add(step, keep, got):
    totals = [k.astype(F32) + g.astype(F32) for k, g in zip(keep, got)]
    if step == 3:
        return [t.astype(BF16) for t in totals], []
    half = totals[0].shape[0] // 2
    return [t[:half].astype(BF16) for t in totals], [t[half:].astype(BF16) for t in totals]


def local(block_input, out_cotangent, w_in, w_out):
    samples, _, width = block_input.shape
    ff = w_out.shape[2]
    x = block_input[:, 0]
    cotangent = out_cotangent[:, 0]
    flat_in = w_in[0].reshape(width, 2 * ff)
    weight_out = w_out[0]
    packed_shape = shape((TOK, samples * 3 // 2, 128))
    index = lax.axis_index("dp").astype(jnp.int32).reshape(1)

    packed = pl.pallas_call(
        pack_kernel, out_shape=packed_shape, in_specs=[VMEM], out_specs=VMEM, compiler_params=params(),
        cost_estimate=cost(samples * width, 4 * samples * width), name="pack",
    )(x)
    recv = lax.all_to_all(packed, "token", split_axis=0, concat_axis=0, tiled=True)

    flat = shape((samples, width))
    own, send, inner, out_grad16 = pl.pallas_call(
        main_kernel,
        out_shape=[shape((width, samples)), shape((width + ff, samples)), shape((2 * ff, samples)), flat],
        in_specs=[SMEM, VMEM, VMEM, ANY, ANY, ANY],
        out_specs=[ANY] * 4,
        scratch_shapes=[
            pltpu.VMEM((width, 2 * ff), BF16),
            pltpu.VMEM((width, ff), BF16),
            pltpu.VMEM((samples, width), BF16),
            pltpu.VMEM((samples, width), BF16),
            pltpu.VMEM((samples, width), BF16),
            pltpu.VMEM((samples, ff), BF16),
            pltpu.VMEM((samples, width), F32),
            pltpu.VMEM((samples, ff), F32),
            pltpu.VMEM((samples, ff), F32),
            pltpu.VMEM((width, samples), BF16),
            pltpu.VMEM((width, samples), BF16),
            pltpu.VMEM((width + ff, samples), BF16),
            pltpu.VMEM((2 * ff, samples), BF16),
            pltpu.SemaphoreType.DMA((8,)),
            pltpu.SemaphoreType.DMA,
            pltpu.SemaphoreType.DMA,
            pltpu.SemaphoreType.DMA((14,)),
        ],
        compiler_params=params(),
        cost_estimate=cost(8 * samples * width * ff, 18e6),
        name="main",
    )(index, x, recv, cotangent, flat_in, weight_out)
    other, inner_other = swap(send, 1), swap(inner, 1)

    up = gradients(True, width // 2, 0, 2 * ff, own, other, inner, inner_other, index, "in_grads")
    up_got = reduce_send((2, 8), 0, up[1::2])
    down = gradients(False, 0, width, ff, own, other, send, other, up[1], "down_grads")
    down_got = reduce_send((8, 2), 0, down[1::2])
    up_keep, down_keep = up[0::2], down[0::2]

    pre_grad, back = pl.pallas_call(
        input_kernel,
        out_shape=[shape((samples, width), F32), packed_shape],
        in_specs=[VMEM, ANY, VMEM, VMEM, VMEM, ANY],
        out_specs=[VMEM] * 2,
        scratch_shapes=[
            pltpu.VMEM((width, 2 * ff), BF16),
            pltpu.VMEM((samples, 2 * ff), BF16),
            pltpu.VMEM((samples, width), F32),
            pltpu.SemaphoreType.DMA((width // 256,)),
        ],
        compiler_params=params(),
        cost_estimate=cost(4 * samples * width * ff, 14e6),
        name="input",
    )(inner, flat_in, x, recv, out_grad16, down[1])
    returned = lax.all_to_all(back, "token", split_axis=0, concat_axis=0, tiled=True)

    for step in range(4):
        if step == 2:
            input_grad = pl.pallas_call(
                final_kernel, out_shape=flat, in_specs=[VMEM] * 2, out_specs=VMEM,
                compiler_params=params(), cost_estimate=cost(samples * width, 8 * samples * width), name="final",
            )(pre_grad, returned)
        up_keep, up_send = reduce_add(step, up_keep, up_got)
        if step < 3:
            up_got = reduce_send((2, 8), step + 1, up_send)
        down_got, up_send = lax.optimization_barrier((down_got, up_send))
        down_keep, down_send = reduce_add(step, down_keep, down_got)
        if step < 3:
            down_got = reduce_send((8, 2), step + 1, down_send)
            up_got, down_send = lax.optimization_barrier((up_got, down_send))

    return (
        input_grad[:, None, :],
        jnp.stack(up_keep, axis=1)[None],
        jnp.concatenate(down_keep, axis=1)[None],
    )


def solution(mesh):
    placed = (
        P("dp", "token", None),
        P("dp", "token", None),
        P("token", None, None, None),
        P("token", None, None),
    )
    return jax.shard_map(
        local,
        mesh=mesh,
        in_specs=placed,
        out_specs=(P("dp", "token", None), P("token", "dp", None, None), P("token", "dp", None)),
        check_vma=False,
    )
```

```python
import functools

import jax
import jax.numpy as jnp
from jax import lax
from jax.experimental import pallas as pl
from jax.experimental.pallas import tpu as pltpu
from jax.sharding import PartitionSpec as P

EPS = 1e-06
TOK = 8
F32 = jnp.float32
BF16 = jnp.bfloat16


def low_lanes(rows):
    return lax.broadcasted_iota(jnp.int32, (rows, 128), 1) < 64


def turn(values):
    return pltpu.roll(values, 64, 1)


def pack(pair, first, middle, last, packed_ref):
    samples = packed_ref.shape[1] * 2 // 3
    half = samples // 2
    low, low_half = low_lanes(samples), low_lanes(half)
    even, odd = packed_ref.at[2 * pair], packed_ref.at[2 * pair + 1]
    even[:samples] = first.astype(BF16)
    even[samples:] = jnp.where(low_half, middle[:half], turn(middle[half:])).astype(BF16)
    odd[:samples] = turn(jnp.where(low, last, middle)).astype(BF16)
    odd[samples:] = jnp.where(low_half, turn(last[:half]), last[half:]).astype(BF16)


def unpack(packed_ref, write):
    samples = packed_ref.shape[1] * 2 // 3
    low = low_lanes(samples)
    for pair in range(TOK // 2):
        even, odd = packed_ref.at[2 * pair], packed_ref.at[2 * pair + 1]
        turned = turn(odd[:samples].astype(F32))
        rest = even[samples:].astype(F32)
        rest = jnp.concatenate([rest, turn(rest)], axis=0)
        rest_odd = odd[samples:].astype(F32)
        rest_odd = jnp.concatenate([turn(rest_odd), rest_odd], axis=0)
        write(3 * pair, even[:samples].astype(F32))
        write(3 * pair + 1, jnp.where(low, rest, turned))
        write(3 * pair + 2, jnp.where(low, turned, rest_odd))


def tile(t):
    return slice(128 * t, 128 * t + 128)


def pack_kernel(x_hbm, packed_hbm, x, packed, in_sem, write_sem):
    def read(pair):
        cols = pl.ds(384 * pair, 384)
        return pltpu.make_async_copy(x_hbm.at[:, cols], x.at[:, cols], in_sem.at[pair])

    def write(pair):
        place = pl.ds(2 * pair, 2)
        return pltpu.make_async_copy(packed.at[place], packed_hbm.at[place], write_sem.at[pair])

    for pair in range(TOK // 2):
        read(pair).start()
    for pair in range(TOK // 2):
        read(pair).wait()
        pack(pair, *(x[:, tile(3 * pair + k)].astype(F32) for k in range(3)), packed)
        write(pair).start()
    for pair in range(TOK // 2):
        write(pair).wait()


def nn(a, b):
    return lax.dot_general(a, b, (((1,), (0,)), ((), ())), preferred_element_type=F32)


def nt(a, b):
    return lax.dot_general(a, b, (((1,), (1,)), ((), ())), preferred_element_type=F32)


def main_kernel(
    index_ref, x_hbm, recv_hbm, cot_hbm, w_in_hbm, w_out_hbm,
    own_hbm, send_hbm, grad16_hbm, normed_hbm, scale_hbm,
    x, recv, w_in, w_out, cot, state, grad16, hidden, normed, scales, values, slope, silu, turned, own, send,
    x_sem, recv_sem, in_sem, out_sem, cot_sem, write_sem,
):
    samples, width = x.shape
    ff = w_out.shape[1]
    wide = 256
    steps = ff // wide
    half = width // 2
    writes = []

    def write(source, target, begin, rows):
        place = pl.ds(begin, rows)
        writes.append(pltpu.make_async_copy(source.at[place], target.at[place], write_sem.at[len(writes)]))
        writes[-1].start()

    def w_in_copy(j, c):
        cols = pl.ds(c * ff + j * wide, wide)
        return pltpu.make_async_copy(w_in_hbm.at[:, cols], w_in.at[:, cols], in_sem.at[2 * j + c])

    x_copy = pltpu.make_async_copy(x_hbm, x, x_sem)
    recv_copy = pltpu.make_async_copy(recv_hbm, recv, recv_sem)
    x_copy.start()
    recv_copy.start()
    for j in range(steps):
        w_in_copy(j, 0).start()
        w_in_copy(j, 1).start()
    out_copy = pltpu.make_async_copy(w_out_hbm, w_out, out_sem)
    out_copy.start()
    cot_copy = pltpu.make_async_copy(cot_hbm, cot, cot_sem)
    cot_copy.start()

    rank = index_ref[0]

    def spread(at):
        for b in range(16):
            place = slice(at + 48 * b, at + 48 * b + 48)
            own[place, :] = turned[pl.ds(pl.multiple_of((rank ^ (2 * b)) * 48, 48), 48), :]
            send[place, :] = turned[pl.ds(pl.multiple_of((rank ^ (2 * b + 1)) * 48, 48), 48), :]
        write(send, send_hbm, at, half)
        write(own, own_hbm, at, half)

    x_copy.wait()
    recv_copy.wait()
    sums = [jnp.zeros((samples, 128), F32)]

    def add_mixed(t, mixed):
        v = x[:, tile(t)].astype(F32) + mixed
        normed[:, tile(t)] = v
        sums[0] = sums[0] + v * v

    unpack(recv, add_mixed)
    scale = lax.rsqrt(jnp.sum(sums[0], axis=1, keepdims=True) / width + EPS)
    scales[...] = jnp.broadcast_to(scale, scales.shape)
    for t in range(width // 128):
        v = normed[:, tile(t)] * scale
        normed[:, tile(t)] = v
        state[:, tile(t)] = v.astype(BF16)
    write(normed, normed_hbm, 0, samples)
    write(scales, scale_hbm, 0, samples)

    for j in range(steps):
        cols = slice(wide * j, wide * j + wide)
        w_in_copy(j, 0).wait()
        gate = nn(state[...], w_in[:, cols])
        w_in_copy(j, 1).wait()
        up = nn(state[...], w_in[:, ff + wide * j : ff + wide * j + wide])
        sigma = jax.nn.sigmoid(gate)
        silu_gate = gate * sigma
        part = (silu_gate * up).astype(BF16)
        hidden[:, cols] = part
        send[width + wide * j : width + wide * j + wide, :] = part
        silu[:, cols] = silu_gate
        slope[:, cols] = up * sigma * (1.0 + gate * (1.0 - sigma))
    write(send, send_hbm, width, ff)

    out_copy.wait()
    for d in range(width // wide):
        cols = slice(wide * d, wide * d + wide)
        values[:, cols] = nt(hidden[...], w_out[cols, :]) + state[:, cols].astype(F32)
    for t in range(width // 128):
        turned[tile(t), :] = state[:, tile(t)].T
    spread(half)
    cot_copy.wait()
    squares = jnp.zeros((samples, 128), F32)
    products = jnp.zeros((samples, 128), F32)
    for t in range(width // 128):
        v = values[:, tile(t)]
        squares = squares + v * v
        products = products + v * cot[:, tile(t)].astype(F32)
    scale = lax.rsqrt(jnp.sum(squares, axis=1, keepdims=True) / width + EPS)
    mean = scale * jnp.sum(products, axis=1, keepdims=True) / width
    for t in range(width // 128):
        out_normed = values[:, tile(t)] * scale
        g16 = (scale * (cot[:, tile(t)].astype(F32) - out_normed * mean)).astype(BF16)
        grad16[:, tile(t)] = g16
        turned[tile(t), :] = g16.T
    write(grad16, grad16_hbm, 0, samples)
    spread(0)
    for j in range(steps):
        cols = slice(wide * j, wide * j + wide)
        hidden_grad = nn(grad16[...], w_out[:, cols])
        at = width + ff + wide * j
        send[at : at + wide, :] = (hidden_grad * slope[:, cols]).astype(BF16)
        send[at + ff : at + ff + wide, :] = (hidden_grad * silu[:, cols]).astype(BF16)
        write(send, send_hbm, at, wide)
        write(send, send_hbm, at + ff, wide)
    for copy in writes:
        copy.wait()


def input_kernel(
    block, send_hbm, w_in_hbm, normed_hbm, scale_hbm, grad_hbm, pre_hbm, packed_hbm,
    w_in, inner, normed, scales, grad, pre, packed, w_sem, inner_sem, side_sem, write_sem,
):
    samples, width = normed.shape
    wide = 256
    reads = []

    def read(source, target, sem):
        reads.append(pltpu.make_async_copy(source, target, sem))
        reads[-1].start()

    for j in range(inner.shape[1] // wide):
        read(send_hbm.at[pl.ds(block + wide * j, wide)], inner.at[:, pl.ds(wide * j, wide)], inner_sem.at[j])
    n_inner = len(reads)
    for d in range(width // wide):
        read(w_in_hbm.at[pl.ds(wide * d, wide)], w_in.at[pl.ds(wide * d, wide)], w_sem.at[d])
        if d == 0:
            read(grad_hbm, grad, side_sem.at[0])
            read(normed_hbm, normed, side_sem.at[1])
            read(scale_hbm, scales, side_sem.at[2])
    waits = [reads[: n_inner + 4]] + [[r] for r in reads[n_inner + 4 :]]
    products = jnp.zeros((samples, 128), F32)
    for d in range(width // wide):
        for copy in waits[d]:
            copy.wait()
        cols = slice(wide * d, wide * d + wide)
        g = nt(inner[...], w_in[cols, :]) + grad[:, cols].astype(F32)
        pre[:, cols] = g
        p = g * normed[:, cols]
        products = products + p[:, :128] + p[:, 128:]
    mean = jnp.sum(products, axis=1, keepdims=True) / width
    scale = scales[:, :1]
    writes = []
    for pair in range(TOK // 2):
        tiles = []
        for t in range(3 * pair, 3 * pair + 3):
            tiles.append(scale * (pre[:, tile(t)] - normed[:, tile(t)] * mean))
            pre[:, tile(t)] = tiles[-1]
        pack(pair, *tiles, packed)
        place, cols = pl.ds(2 * pair, 2), pl.ds(384 * pair, 384)
        writes.append(pltpu.make_async_copy(packed.at[place], packed_hbm.at[place], write_sem.at[2 * pair]))
        writes.append(pltpu.make_async_copy(pre.at[:, cols], pre_hbm.at[:, cols], write_sem.at[2 * pair + 1]))
        writes[-2].start()
        writes[-1].start()
    for copy in writes:
        copy.wait()


def final_kernel(pre_ref, recv_ref, out_ref):
    def write(t, returned):
        out_ref[:, tile(t)] = (pre_ref[:, tile(t)] + returned).astype(BF16)

    unpack(recv_ref, write)


KEEP_FIRST = ((0, 3, 1, 2), (0, 1, 3, 2))
PARTNERS = ((1, 3), (3, 1))


def grad_kernel(x_first, at, block, own_hbm, send_hbm, other_hbm, after_hbm, *refs):
    del after_hbm
    outs_hbm, outs = refs[:4], refs[4:8]
    own, other, right, right_other, in_sem, write_sem = refs[8:]
    rows = own.shape[0]
    wide = 256
    per = outs[0].shape[1] // wide
    reads, writes = [], []

    def read(source, begin, target, to, count):
        copy = pltpu.make_async_copy(
            source.at[pl.ds(begin, count)], target.at[pl.ds(to, count)], in_sem.at[len(reads)]
        )
        copy.start()
        reads.append(copy)

    read(own_hbm, at, own, 0, rows)
    read(other_hbm, at, other, 0, rows)
    for k in range(2 * per):
        read(send_hbm, block + wide * k, right, wide * k, wide)
        read(other_hbm, block + wide * k, right_other, wide * k, wide)
    reads[0].wait()
    reads[1].wait()
    for k in range(2 * per):
        flavour, col = divmod(k, per)
        keep, send = outs[2 * flavour], outs[2 * flavour + 1]
        order = KEEP_FIRST[flavour]
        reads[2 + 2 * k].wait()
        reads[3 + 2 * k].wait()
        place, cols = slice(wide * k, wide * k + wide), slice(wide * col, wide * col + wide)
        g = (nn(own[...], right[place, :]) + nn(other[...], right_other[place, :])).astype(BF16)
        for b in range(16):
            rz, rx = order.index(b // 4), order.index(b % 4)
            to = rx * 4 + rz if x_first else rz * 4 + rx
            target = keep if to < 8 else send
            to = (to % 8) * 48
            target[to : to + 48, cols] = g[48 * b : 48 * b + 48]
        for side in range(2):
            n = 2 * flavour + side
            cols = pl.ds(wide * col, wide)
            copy = pltpu.make_async_copy(outs[n].at[:, cols], outs_hbm[n].at[:, cols], write_sem.at[len(writes)])
            copy.start()
            writes.append(copy)
    for copy in writes:
        copy.wait()


def params(mebibytes):
    return pltpu.CompilerParams(vmem_limit_bytes=mebibytes * 1024 * 1024)


VMEM = pl.BlockSpec(memory_space=pltpu.VMEM)
SMEM = pl.BlockSpec(memory_space=pltpu.SMEM)
ANY = pl.BlockSpec(memory_space=pl.ANY)


def cost(flops, moved):
    return pl.CostEstimate(flops=int(flops), bytes_accessed=int(moved), transcendentals=0)


def shape(dims, dtype=BF16):
    return jax.ShapeDtypeStruct(dims, dtype)


def swap(values, distance):
    return lax.ppermute(values, "dp", [(i, i ^ distance) for i in range(32)])


def gradients(x_first, at, block, columns, own, send, other, after, name):
    piece = shape((384, columns // 2))
    rows, samples = own.shape[0] // 2, own.shape[1]
    moved = (2 * rows * samples + 2 * samples * columns + rows * columns) * 2
    return pl.pallas_call(
        functools.partial(grad_kernel, x_first, at, block),
        out_shape=[piece] * 4,
        in_specs=[ANY] * 4,
        out_specs=[ANY] * 4,
        scratch_shapes=[pltpu.VMEM(piece.shape, BF16)] * 4
        + [pltpu.VMEM((rows, samples), BF16)] * 2
        + [pltpu.VMEM((columns, samples), BF16)] * 2
        + [pltpu.SemaphoreType.DMA((2 + columns // 128,)), pltpu.SemaphoreType.DMA((columns // 128,))],
        compiler_params=params(56),
        cost_estimate=cost(2 * rows * 2 * samples * columns, moved),
        name=name,
    )(own, send, other, after)


def reduce_send(scales, step, send):
    return [swap(send[f], PARTNERS[f][step % 2] * scales[step // 2]) for f in range(2)]


def reduce_add(step, keep, got):
    totals = [k.astype(F32) + g.astype(F32) for k, g in zip(keep, got)]
    if step == 3:
        return [t.astype(BF16) for t in totals], []
    half = totals[0].shape[0] // 2
    return [t[:half].astype(BF16) for t in totals], [t[half:].astype(BF16) for t in totals]


def local(block_input, out_cotangent, w_in, w_out):
    samples, _, width = block_input.shape
    ff = w_out.shape[2]
    x = block_input[:, 0]
    cotangent = out_cotangent[:, 0]
    flat_in = w_in[0].reshape(width, 2 * ff)
    weight_out = w_out[0]
    packed_shape = shape((TOK, samples * 3 // 2, 128))
    index = lax.axis_index("dp").astype(jnp.int32).reshape(1)

    packed = pl.pallas_call(
        pack_kernel, out_shape=packed_shape, in_specs=[ANY], out_specs=ANY, compiler_params=params(56),
        scratch_shapes=[
            pltpu.VMEM((samples, width), BF16),
            pltpu.VMEM(packed_shape.shape, BF16),
            pltpu.SemaphoreType.DMA((4,)),
            pltpu.SemaphoreType.DMA((4,)),
        ],
        cost_estimate=cost(samples * width, 4 * samples * width), name="pack",
    )(x)
    recv = lax.all_to_all(packed, "token", split_axis=0, concat_axis=0, tiled=True)

    flat = shape((samples, width))
    full, scales = shape((samples, width), F32), shape((samples, 128), F32)
    own, send, out_grad16, normed, scale = pl.pallas_call(
        main_kernel,
        out_shape=[shape((width, samples)), shape((width + 3 * ff, samples)), flat, full, scales],
        in_specs=[SMEM] + [ANY] * 5,
        out_specs=[ANY] * 5,
        scratch_shapes=[
            pltpu.VMEM((samples, width), BF16),
            pltpu.VMEM(packed_shape.shape, BF16),
            pltpu.VMEM((width, 2 * ff), BF16),
            pltpu.VMEM((width, ff), BF16),
            pltpu.VMEM((samples, width), BF16),
            pltpu.VMEM((samples, width), BF16),
            pltpu.VMEM((samples, width), BF16),
            pltpu.VMEM((samples, ff), BF16),
            pltpu.VMEM((samples, width), F32),
            pltpu.VMEM((samples, 128), F32),
            pltpu.VMEM((samples, width), F32),
            pltpu.VMEM((samples, ff), F32),
            pltpu.VMEM((samples, ff), F32),
            pltpu.VMEM((width, samples), BF16),
            pltpu.VMEM((width, samples), BF16),
            pltpu.VMEM((width + 3 * ff, samples), BF16),
            pltpu.SemaphoreType.DMA,
            pltpu.SemaphoreType.DMA,
            pltpu.SemaphoreType.DMA((8,)),
            pltpu.SemaphoreType.DMA,
            pltpu.SemaphoreType.DMA,
            pltpu.SemaphoreType.DMA((16,)),
        ],
        compiler_params=params(56),
        cost_estimate=cost(8 * samples * width * ff, 18e6),
        name="main",
    )(index, x, recv, cotangent, flat_in, weight_out)
    other = swap(send, 1)

    pre_grad, back = pl.pallas_call(
        functools.partial(input_kernel, width + ff),
        out_shape=[full, packed_shape],
        in_specs=[ANY] * 5,
        out_specs=[ANY] * 2,
        scratch_shapes=[
            pltpu.VMEM((width, 2 * ff), BF16),
            pltpu.VMEM((samples, 2 * ff), BF16),
            pltpu.VMEM((samples, width), F32),
            pltpu.VMEM((samples, 128), F32),
            pltpu.VMEM((samples, width), BF16),
            pltpu.VMEM((samples, width), F32),
            pltpu.VMEM(packed_shape.shape, BF16),
            pltpu.SemaphoreType.DMA((width // 256,)),
            pltpu.SemaphoreType.DMA((8,)),
            pltpu.SemaphoreType.DMA((3,)),
            pltpu.SemaphoreType.DMA((8,)),
        ],
        compiler_params=params(56),
        cost_estimate=cost(4 * samples * width * ff, 14e6),
        name="input",
    )(send, flat_in, normed, scale, out_grad16)

    up = gradients(True, width // 2, width + ff, 2 * ff, own, send, other, back, "in_grads")
    up_got = reduce_send((2, 8), 0, up[1::2])
    down = gradients(False, 0, width, ff, own, send, other, up[1], "down_grads")
    down_got = reduce_send((8, 2), 0, down[1::2])
    up_keep, down_keep = up[0::2], down[0::2]
    returned = lax.all_to_all(back, "token", split_axis=0, concat_axis=0, tiled=True)

    for step in range(4):
        if step == 2:
            input_grad = pl.pallas_call(
                final_kernel, out_shape=flat, in_specs=[VMEM] * 2, out_specs=VMEM,
                compiler_params=params(56), cost_estimate=cost(samples * width, 8 * samples * width), name="final",
            )(pre_grad, returned)
        up_keep, up_send = reduce_add(step, up_keep, up_got)
        if step < 3:
            up_got = reduce_send((2, 8), step + 1, up_send)
        down_got, up_send = lax.optimization_barrier((down_got, up_send))
        down_keep, down_send = reduce_add(step, down_keep, down_got)
        if step < 3:
            down_got = reduce_send((8, 2), step + 1, down_send)
            up_got, down_send = lax.optimization_barrier((up_got, down_send))

    return (
        input_grad[:, None, :],
        jnp.stack(up_keep, axis=1)[None],
        jnp.concatenate(down_keep, axis=1)[None],
    )


def solution(mesh):
    placed = (
        P("dp", "token", None),
        P("dp", "token", None),
        P("token", None, None, None),
        P("token", None, None),
    )
    return jax.shard_map(
        local,
        mesh=mesh,
        in_specs=placed,
        out_specs=(P("dp", "token", None), P("token", "dp", None, None), P("token", "dp", None)),
        check_vma=False,
    )
```

```python
import functools

import jax
import jax.numpy as jnp
from jax import lax
from jax.experimental import pallas as pl
from jax.experimental.pallas import tpu as pltpu
from jax.sharding import PartitionSpec as P

EPS = 1e-06
TOK = 8
F32 = jnp.float32
BF16 = jnp.bfloat16
VMEM_LIMIT = 56 * 1024 * 1024


def low_lanes(rows):
    return lax.broadcasted_iota(jnp.int32, (rows, 128), 1) < 64


def turn(values):
    return pltpu.roll(values, 64, 1)


def pack(read, packed_ref):
    samples = packed_ref.shape[1] * 2 // 3
    half = samples // 2
    low, low_half = low_lanes(samples), low_lanes(half)
    for pair in range(TOK // 2):
        first, middle, last = read(3 * pair), read(3 * pair + 1), read(3 * pair + 2)
        even, odd = packed_ref.at[2 * pair], packed_ref.at[2 * pair + 1]
        even[:samples] = first.astype(BF16)
        even[samples:] = jnp.where(low_half, middle[:half], turn(middle[half:])).astype(BF16)
        odd[:samples] = turn(jnp.where(low, last, middle)).astype(BF16)
        odd[samples:] = jnp.where(low_half, turn(last[:half]), last[half:]).astype(BF16)


def unpack(packed_ref, write):
    samples = packed_ref.shape[1] * 2 // 3
    low = low_lanes(samples)
    for pair in range(TOK // 2):
        even, odd = packed_ref.at[2 * pair], packed_ref.at[2 * pair + 1]
        turned = turn(odd[:samples].astype(F32))
        rest = even[samples:].astype(F32)
        rest = jnp.concatenate([rest, turn(rest)], axis=0)
        rest_odd = odd[samples:].astype(F32)
        rest_odd = jnp.concatenate([turn(rest_odd), rest_odd], axis=0)
        write(3 * pair, even[:samples].astype(F32))
        write(3 * pair + 1, jnp.where(low, rest, turned))
        write(3 * pair + 2, jnp.where(low, turned, rest_odd))


def tile(t):
    return slice(128 * t, 128 * t + 128)


def pack_kernel(x_ref, packed_ref):
    pack(lambda t: x_ref[:, tile(t)].astype(F32), packed_ref)


def nn(a, b):
    return lax.dot_general(a, b, (((1,), (0,)), ((), ())), preferred_element_type=F32)


def nt(a, b):
    return lax.dot_general(a, b, (((1,), (1,)), ((), ())), preferred_element_type=F32)


def norm_state(x_ref, recv_ref, normed_ref):
    samples, width = x_ref.shape
    sums = [jnp.zeros((samples, 128), F32)]

    def add_mixed(t, mixed):
        v = x_ref[:, tile(t)].astype(F32) + mixed
        normed_ref[:, tile(t)] = v
        sums[0] = sums[0] + v * v

    unpack(recv_ref, add_mixed)
    scale = lax.rsqrt(jnp.sum(sums[0], axis=1, keepdims=True) / width + EPS)
    for t in range(width // 128):
        normed_ref[:, tile(t)] = normed_ref[:, tile(t)] * scale
    return scale


def main_kernel(
    index_ref, x_ref, recv_ref, cot_hbm, w_in_hbm, w_out_hbm,
    own_hbm, send_hbm, inner_hbm, grad16_hbm,
    w_in, w_out, cot, state, grad16, hidden, values, slope, silu, turned, own, send, inner,
    in_sem, out_sem, cot_sem, write_sem,
):
    samples, width = x_ref.shape
    ff = w_out.shape[1]
    wide = 256
    steps = ff // wide
    half = width // 2
    writes = []

    def write(source, target, begin, rows):
        place = pl.ds(begin, rows)
        writes.append(pltpu.make_async_copy(source.at[place], target.at[place], write_sem.at[len(writes)]))
        writes[-1].start()

    def w_in_copy(j, c):
        cols = pl.ds(c * ff + j * wide, wide)
        return pltpu.make_async_copy(w_in_hbm.at[:, cols], w_in.at[:, cols], in_sem.at[2 * j + c])

    for j in range(steps):
        w_in_copy(j, 0).start()
        w_in_copy(j, 1).start()
    out_copy = pltpu.make_async_copy(w_out_hbm, w_out, out_sem)
    out_copy.start()
    cot_copy = pltpu.make_async_copy(cot_hbm, cot, cot_sem)
    cot_copy.start()

    rank = index_ref[0]

    def spread(at):
        for b in range(16):
            place = slice(at + 48 * b, at + 48 * b + 48)
            own[place, :] = turned[pl.ds(pl.multiple_of((rank ^ (2 * b)) * 48, 48), 48), :]
            send[place, :] = turned[pl.ds(pl.multiple_of((rank ^ (2 * b + 1)) * 48, 48), 48), :]
        write(send, send_hbm, at, half)
        write(own, own_hbm, at, half)

    norm_state(x_ref, recv_ref, values)
    for t in range(width // 128):
        state[:, tile(t)] = values[:, tile(t)].astype(BF16)

    for j in range(steps):
        cols = slice(wide * j, wide * j + wide)
        w_in_copy(j, 0).wait()
        gate = nn(state[...], w_in[:, cols])
        w_in_copy(j, 1).wait()
        up = nn(state[...], w_in[:, ff + wide * j : ff + wide * j + wide])
        sigma = jax.nn.sigmoid(gate)
        silu_gate = gate * sigma
        part = (silu_gate * up).astype(BF16)
        hidden[:, cols] = part
        send[width + wide * j : width + wide * j + wide, :] = part
        silu[:, cols] = silu_gate
        slope[:, cols] = up * sigma * (1.0 + gate * (1.0 - sigma))
    write(send, send_hbm, width, ff)

    out_copy.wait()
    for d in range(width // wide):
        cols = slice(wide * d, wide * d + wide)
        values[:, cols] = nt(hidden[...], w_out[cols, :]) + state[:, cols].astype(F32)
    for t in range(width // 128):
        turned[tile(t), :] = state[:, tile(t)].T
    spread(half)
    cot_copy.wait()
    squares = jnp.zeros((samples, 128), F32)
    products = jnp.zeros((samples, 128), F32)
    for t in range(width // 128):
        v = values[:, tile(t)]
        squares = squares + v * v
        products = products + v * cot[:, tile(t)].astype(F32)
    scale = lax.rsqrt(jnp.sum(squares, axis=1, keepdims=True) / width + EPS)
    mean = scale * jnp.sum(products, axis=1, keepdims=True) / width
    for t in range(width // 128):
        out_normed = values[:, tile(t)] * scale
        g16 = (scale * (cot[:, tile(t)].astype(F32) - out_normed * mean)).astype(BF16)
        grad16[:, tile(t)] = g16
        turned[tile(t), :] = g16.T
    write(grad16, grad16_hbm, 0, samples)
    spread(0)
    for j in range(steps):
        cols = slice(wide * j, wide * j + wide)
        hidden_grad = nn(grad16[...], w_out[:, cols])
        inner[cols, :] = (hidden_grad * slope[:, cols]).astype(BF16)
        inner[ff + wide * j : ff + wide * j + wide, :] = (hidden_grad * silu[:, cols]).astype(BF16)
        write(inner, inner_hbm, wide * j, wide)
        write(inner, inner_hbm, ff + wide * j, wide)
    for copy in writes:
        copy.wait()


def input_kernel(
    inner_ref, w_in_hbm, x_ref, recv_ref, grad_ref, after_ref, pre_ref, packed_ref, w_in, inner, normed, sem
):
    del after_ref
    samples, width = x_ref.shape
    wide = 256

    def copy(d):
        rows = pl.ds(d * wide, wide)
        return pltpu.make_async_copy(w_in_hbm.at[rows], w_in.at[rows], sem.at[d])

    for d in range(width // wide):
        copy(d).start()
    scale = norm_state(x_ref, recv_ref, normed)
    for j in range(inner.shape[1] // samples):
        inner[:, samples * j : samples * j + samples] = inner_ref[samples * j : samples * j + samples, :]
    products = jnp.zeros((samples, 128), F32)
    for d in range(width // wide):
        copy(d).wait()
        cols = slice(wide * d, wide * d + wide)
        g = nt(inner[...], w_in[cols, :]) + grad_ref[:, cols].astype(F32)
        pre_ref[:, cols] = g
        p = g * normed[:, cols]
        products = products + p[:, :128] + p[:, 128:]
    mean = jnp.sum(products, axis=1, keepdims=True) / width
    for t in range(width // 128):
        pre_ref[:, tile(t)] = scale * (pre_ref[:, tile(t)] - normed[:, tile(t)] * mean)
    pack(lambda t: pre_ref[:, tile(t)], packed_ref)


def final_kernel(pre_ref, recv_ref, out_ref):
    def write(t, returned):
        out_ref[:, tile(t)] = (pre_ref[:, tile(t)] + returned).astype(BF16)

    unpack(recv_ref, write)


KEEP_FIRST = ((0, 3, 1, 2), (0, 1, 3, 2))
PARTNERS = ((1, 3), (3, 1))
SCALES = (2, 2, 8, 8)


def grad_kernel(at, block, own_hbm, other_hbm, right_hbm, right_other_hbm, after_hbm, *refs):
    del after_hbm
    outs_hbm, outs = refs[:4], refs[4:8]
    own, other, right, right_other, in_sem, write_sem = refs[8:]
    wide = 256
    per = outs[0].shape[1] // wide
    sources = ((own_hbm, at, own), (other_hbm, at, other), (right_hbm, block, right), (right_other_hbm, block, right_other))
    reads, writes = [], []
    for n, (source, begin, target) in enumerate(sources):
        reads.append(pltpu.make_async_copy(source.at[pl.ds(begin, target.shape[0])], target, in_sem.at[n]))
        reads[-1].start()
    for copy in reads:
        copy.wait()
    for flavour in range(2):
        keep, send = outs[2 * flavour], outs[2 * flavour + 1]
        order = KEEP_FIRST[flavour]
        for col in range(per):
            k = flavour * per + col
            place, cols = slice(wide * k, wide * k + wide), slice(wide * col, wide * col + wide)
            g = (nn(own[...], right[place, :]) + nn(other[...], right_other[place, :])).astype(BF16)
            for b in range(16):
                to = order.index(b % 4) * 4 + order.index(b // 4)
                target = keep if to < 8 else send
                to = (to % 8) * 48
                target[to : to + 48, cols] = g[48 * b : 48 * b + 48]
        for n in (2 * flavour, 2 * flavour + 1):
            writes.append(pltpu.make_async_copy(outs[n], outs_hbm[n], write_sem.at[n]))
            writes[-1].start()
    for copy in writes:
        copy.wait()


def params():
    return pltpu.CompilerParams(vmem_limit_bytes=VMEM_LIMIT)


VMEM = pl.BlockSpec(memory_space=pltpu.VMEM)
SMEM = pl.BlockSpec(memory_space=pltpu.SMEM)
ANY = pl.BlockSpec(memory_space=pl.ANY)


def cost(flops, moved):
    return pl.CostEstimate(flops=int(flops), bytes_accessed=int(moved), transcendentals=0)


def shape(dims, dtype=BF16):
    return jax.ShapeDtypeStruct(dims, dtype)


def swap(values, distance):
    return lax.ppermute(values, "dp", [(i, i ^ distance) for i in range(32)])


def gradients(at, block, columns, own, other, right, right_other, after, name):
    piece = shape((384, columns // 2))
    rows, samples = own.shape[0] // 2, own.shape[1]
    moved = (2 * rows * samples + 2 * samples * columns + rows * columns) * 2
    return pl.pallas_call(
        functools.partial(grad_kernel, at, block),
        out_shape=[piece] * 4,
        in_specs=[ANY] * 5,
        out_specs=[ANY] * 4,
        scratch_shapes=[pltpu.VMEM(piece.shape, BF16)] * 4
        + [pltpu.VMEM((rows, samples), BF16)] * 2
        + [pltpu.VMEM((columns, samples), BF16)] * 2
        + [pltpu.SemaphoreType.DMA((4,))] * 2,
        compiler_params=params(),
        cost_estimate=cost(2 * rows * 2 * samples * columns, moved),
        name=name,
    )(own, other, right, right_other, after)


def reduce_send(step, send):
    return [swap(send[f], PARTNERS[f][step % 2] * SCALES[step]) for f in range(2)]


def reduce_add(step, keep, got):
    totals = [k.astype(F32) + g.astype(F32) for k, g in zip(keep, got)]
    if step == 3:
        return [t.astype(BF16) for t in totals], []
    half = totals[0].shape[0] // 2
    return [t[:half].astype(BF16) for t in totals], [t[half:].astype(BF16) for t in totals]


def local(block_input, out_cotangent, w_in, w_out):
    samples, _, width = block_input.shape
    ff = w_out.shape[2]
    x = block_input[:, 0]
    cotangent = out_cotangent[:, 0]
    flat_in = w_in[0].reshape(width, 2 * ff)
    weight_out = w_out[0]
    packed_shape = shape((TOK, samples * 3 // 2, 128))
    index = lax.axis_index("dp").astype(jnp.int32).reshape(1)

    packed = pl.pallas_call(
        pack_kernel, out_shape=packed_shape, in_specs=[VMEM], out_specs=VMEM, compiler_params=params(),
        cost_estimate=cost(samples * width, 4 * samples * width), name="pack",
    )(x)
    recv = lax.all_to_all(packed, "token", split_axis=0, concat_axis=0, tiled=True)

    flat = shape((samples, width))
    own, send, inner, out_grad16 = pl.pallas_call(
        main_kernel,
        out_shape=[shape((width, samples)), shape((width + ff, samples)), shape((2 * ff, samples)), flat],
        in_specs=[SMEM, VMEM, VMEM, ANY, ANY, ANY],
        out_specs=[ANY] * 4,
        scratch_shapes=[
            pltpu.VMEM((width, 2 * ff), BF16),
            pltpu.VMEM((width, ff), BF16),
            pltpu.VMEM((samples, width), BF16),
            pltpu.VMEM((samples, width), BF16),
            pltpu.VMEM((samples, width), BF16),
            pltpu.VMEM((samples, ff), BF16),
            pltpu.VMEM((samples, width), F32),
            pltpu.VMEM((samples, ff), F32),
            pltpu.VMEM((samples, ff), F32),
            pltpu.VMEM((width, samples), BF16),
            pltpu.VMEM((width, samples), BF16),
            pltpu.VMEM((width + ff, samples), BF16),
            pltpu.VMEM((2 * ff, samples), BF16),
            pltpu.SemaphoreType.DMA((8,)),
            pltpu.SemaphoreType.DMA,
            pltpu.SemaphoreType.DMA,
            pltpu.SemaphoreType.DMA((14,)),
        ],
        compiler_params=params(),
        cost_estimate=cost(8 * samples * width * ff, 18e6),
        name="main",
    )(index, x, recv, cotangent, flat_in, weight_out)
    other, inner_other = swap(send, 1), swap(inner, 1)

    half = width // 2
    down = gradients(0, width, ff, own, other, send, other, inner, "down_grads")
    gate = gradients(half, 0, ff, own, other, inner, inner_other, down[1], "gate_grads")
    up = gradients(half, ff, ff, own, other, inner, inner_other, gate[1], "up_grads")
    kept = [grads[0::2] for grads in (down, gate, up)]
    got = [reduce_send(0, grads[1::2]) for grads in (down, gate, up)]

    pre_grad, back = pl.pallas_call(
        input_kernel,
        out_shape=[shape((samples, width), F32), packed_shape],
        in_specs=[VMEM, ANY, VMEM, VMEM, VMEM, ANY],
        out_specs=[VMEM] * 2,
        scratch_shapes=[
            pltpu.VMEM((width, 2 * ff), BF16),
            pltpu.VMEM((samples, 2 * ff), BF16),
            pltpu.VMEM((samples, width), F32),
            pltpu.SemaphoreType.DMA((width // 256,)),
        ],
        compiler_params=params(),
        cost_estimate=cost(4 * samples * width * ff, 14e6),
        name="input",
    )(inner, flat_in, x, recv, out_grad16, up[1])
    returned = lax.all_to_all(back, "token", split_axis=0, concat_axis=0, tiled=True)

    input_grad = pl.pallas_call(
        final_kernel, out_shape=flat, in_specs=[VMEM] * 2, out_specs=VMEM,
        compiler_params=params(), cost_estimate=cost(samples * width, 8 * samples * width), name="final",
    )(pre_grad, returned)

    previous = None
    for which, step in ((0, 0), (1, 0), (0, 1), (2, 0), (1, 1), (0, 2), (2, 1), (1, 2), (0, 3), (2, 2), (1, 3), (2, 3)):
        arrived = got[which]
        if previous is not None:
            arrived, previous = lax.optimization_barrier((arrived, previous))
        if (which, step) == (0, 3):
            arrived, input_grad = lax.optimization_barrier((arrived, input_grad))
        kept[which], sent = reduce_add(step, kept[which], arrived)
        previous = sent or kept[which]
        if step < 3:
            got[which] = reduce_send(step + 1, sent)

    down, gate, up = (jnp.concatenate(k, axis=1) for k in kept)
    return (input_grad[:, None, :], jnp.stack([gate, up], axis=1)[None], down[None])


def solution(mesh):
    placed = (
        P("dp", "token", None),
        P("dp", "token", None),
        P("token", None, None, None),
        P("token", None, None),
    )
    return jax.shard_map(
        local,
        mesh=mesh,
        in_specs=placed,
        out_specs=(P("dp", "token", None), P("token", "dp", None, None), P("token", "dp", None)),
        check_vma=False,
    )
```

```python
import functools

import jax
import jax.numpy as jnp
from jax import lax
from jax.experimental import pallas as pl
from jax.experimental.pallas import tpu as pltpu
from jax.sharding import PartitionSpec as P

EPS = 1e-06
TOK = 8
F32 = jnp.float32
BF16 = jnp.bfloat16
VMEM_LIMIT = 56 * 1024 * 1024


def low_lanes(rows):
    return lax.broadcasted_iota(jnp.int32, (rows, 128), 1) < 64


def turn(values):
    return pltpu.roll(values, 64, 1)


def pack(read, packed_ref):
    samples = packed_ref.shape[1] * 2 // 3
    half = samples // 2
    low, low_half = low_lanes(samples), low_lanes(half)
    for pair in range(TOK // 2):
        first, middle, last = read(3 * pair), read(3 * pair + 1), read(3 * pair + 2)
        even, odd = packed_ref.at[2 * pair], packed_ref.at[2 * pair + 1]
        even[:samples] = first.astype(BF16)
        even[samples:] = jnp.where(low_half, middle[:half], turn(middle[half:])).astype(BF16)
        odd[:samples] = turn(jnp.where(low, last, middle)).astype(BF16)
        odd[samples:] = jnp.where(low_half, turn(last[:half]), last[half:]).astype(BF16)


def unpack(packed_ref, write):
    samples = packed_ref.shape[1] * 2 // 3
    low = low_lanes(samples)
    for pair in range(TOK // 2):
        even, odd = packed_ref.at[2 * pair], packed_ref.at[2 * pair + 1]
        turned = turn(odd[:samples].astype(F32))
        rest = even[samples:].astype(F32)
        rest = jnp.concatenate([rest, turn(rest)], axis=0)
        rest_odd = odd[samples:].astype(F32)
        rest_odd = jnp.concatenate([turn(rest_odd), rest_odd], axis=0)
        write(3 * pair, even[:samples].astype(F32))
        write(3 * pair + 1, jnp.where(low, rest, turned))
        write(3 * pair + 2, jnp.where(low, turned, rest_odd))


def tile(t):
    return slice(128 * t, 128 * t + 128)


def pack_kernel(x_ref, packed_ref):
    pack(lambda t: x_ref[:, tile(t)].astype(F32), packed_ref)


def nn(a, b):
    return lax.dot_general(a, b, (((1,), (0,)), ((), ())), preferred_element_type=F32)


def nt(a, b):
    return lax.dot_general(a, b, (((1,), (1,)), ((), ())), preferred_element_type=F32)


def norm_state(x_ref, recv_ref, normed_ref):
    samples, width = x_ref.shape
    sums = [jnp.zeros((samples, 128), F32)]

    def add_mixed(t, mixed):
        v = x_ref[:, tile(t)].astype(F32) + mixed
        normed_ref[:, tile(t)] = v
        sums[0] = sums[0] + v * v

    unpack(recv_ref, add_mixed)
    scale = lax.rsqrt(jnp.sum(sums[0], axis=1, keepdims=True) / width + EPS)
    for t in range(width // 128):
        normed_ref[:, tile(t)] = normed_ref[:, tile(t)] * scale
    return scale


def main_kernel(
    index_ref, x_ref, recv_ref, cot_hbm, w_in_hbm, w_out_hbm,
    own_hbm, send_hbm, inner_hbm, grad16_hbm,
    w_in, w_out, cot, state, grad16, hidden, values, slope, silu, turned, own, send, inner,
    in_sem, out_sem, cot_sem, write_sem,
):
    samples, width = x_ref.shape
    ff = w_out.shape[1]
    wide = 256
    steps = ff // wide
    half = width // 2
    writes = []

    def write(source, target, begin, rows):
        place = pl.ds(begin, rows)
        writes.append(pltpu.make_async_copy(source.at[place], target.at[place], write_sem.at[len(writes)]))
        writes[-1].start()

    def w_in_copy(j, c):
        cols = pl.ds(c * ff + j * wide, wide)
        return pltpu.make_async_copy(w_in_hbm.at[:, cols], w_in.at[:, cols], in_sem.at[2 * j + c])

    for j in range(steps):
        w_in_copy(j, 0).start()
        w_in_copy(j, 1).start()
    out_copy = pltpu.make_async_copy(w_out_hbm, w_out, out_sem)
    out_copy.start()
    cot_copy = pltpu.make_async_copy(cot_hbm, cot, cot_sem)
    cot_copy.start()

    rank = index_ref[0]

    def block(place, flavour):
        rx, rz = ((0, 3 - 2 * flavour, 1 + 2 * flavour, 2)[at] for at in divmod(place, 4))
        return 4 * rz + rx

    core = rank & 1

    def spread(at):
        for p in range(16):
            place = slice(at + 48 * p, at + 48 * p + 48)
            mine = (rank ^ (2 * block(p, core))) * 48
            theirs = (rank ^ (2 * block(p, 1 - core) + 1)) * 48
            own[place, :] = turned[pl.ds(pl.multiple_of(mine, 48), 48), :]
            send[place, :] = turned[pl.ds(pl.multiple_of(theirs, 48), 48), :]
        write(send, send_hbm, at, half)
        write(own, own_hbm, at, half)

    norm_state(x_ref, recv_ref, values)
    for t in range(width // 128):
        state[:, tile(t)] = values[:, tile(t)].astype(BF16)

    for j in range(steps):
        cols = slice(wide * j, wide * j + wide)
        w_in_copy(j, 0).wait()
        gate = nn(state[...], w_in[:, cols])
        w_in_copy(j, 1).wait()
        up = nn(state[...], w_in[:, ff + wide * j : ff + wide * j + wide])
        sigma = jax.nn.sigmoid(gate)
        silu_gate = gate * sigma
        part = (silu_gate * up).astype(BF16)
        hidden[:, cols] = part
        send[width + wide * j : width + wide * j + wide, :] = part
        silu[:, cols] = silu_gate
        slope[:, cols] = up * sigma * (1.0 + gate * (1.0 - sigma))
    write(send, send_hbm, width, ff)

    out_copy.wait()
    for d in range(width // wide):
        cols = slice(wide * d, wide * d + wide)
        values[:, cols] = nt(hidden[...], w_out[cols, :]) + state[:, cols].astype(F32)
    for t in range(width // 128):
        turned[tile(t), :] = state[:, tile(t)].T
    spread(half)
    cot_copy.wait()
    squares = jnp.zeros((samples, 128), F32)
    products = jnp.zeros((samples, 128), F32)
    for t in range(width // 128):
        v = values[:, tile(t)]
        squares = squares + v * v
        products = products + v * cot[:, tile(t)].astype(F32)
    scale = lax.rsqrt(jnp.sum(squares, axis=1, keepdims=True) / width + EPS)
    mean = scale * jnp.sum(products, axis=1, keepdims=True) / width
    for t in range(width // 128):
        out_normed = values[:, tile(t)] * scale
        g16 = (scale * (cot[:, tile(t)].astype(F32) - out_normed * mean)).astype(BF16)
        grad16[:, tile(t)] = g16
        turned[tile(t), :] = g16.T
    write(grad16, grad16_hbm, 0, samples)
    spread(0)
    for j in range(steps):
        cols = slice(wide * j, wide * j + wide)
        hidden_grad = nn(grad16[...], w_out[:, cols])
        inner[cols, :] = (hidden_grad * slope[:, cols]).astype(BF16)
        inner[ff + wide * j : ff + wide * j + wide, :] = (hidden_grad * silu[:, cols]).astype(BF16)
        write(inner, inner_hbm, wide * j, wide)
        write(inner, inner_hbm, ff + wide * j, wide)
    for copy in writes:
        copy.wait()


def input_kernel(
    inner_ref, w_in_hbm, x_ref, recv_ref, grad_ref, after_ref, pre_ref, packed_ref, w_in, inner, normed, sem
):
    del after_ref
    samples, width = x_ref.shape
    wide = 256

    def copy(d):
        rows = pl.ds(d * wide, wide)
        return pltpu.make_async_copy(w_in_hbm.at[rows], w_in.at[rows], sem.at[d])

    for d in range(width // wide):
        copy(d).start()
    scale = norm_state(x_ref, recv_ref, normed)
    for j in range(inner.shape[1] // samples):
        inner[:, samples * j : samples * j + samples] = inner_ref[samples * j : samples * j + samples, :]
    products = jnp.zeros((samples, 128), F32)
    for d in range(width // wide):
        copy(d).wait()
        cols = slice(wide * d, wide * d + wide)
        g = nt(inner[...], w_in[cols, :]) + grad_ref[:, cols].astype(F32)
        pre_ref[:, cols] = g
        p = g * normed[:, cols]
        products = products + p[:, :128] + p[:, 128:]
    mean = jnp.sum(products, axis=1, keepdims=True) / width
    for t in range(width // 128):
        pre_ref[:, tile(t)] = scale * (pre_ref[:, tile(t)] - normed[:, tile(t)] * mean)
    pack(lambda t: pre_ref[:, tile(t)], packed_ref)


def final_kernel(pre_ref, recv_ref, out_ref):
    def write(t, returned):
        out_ref[:, tile(t)] = (pre_ref[:, tile(t)] + returned).astype(BF16)

    unpack(recv_ref, write)


PARTNERS = ((1, 3), (3, 1))
SCALES = (2, 2, 8, 8)


def grad_kernel(at, block, own_hbm, other_hbm, right_hbm, right_other_hbm, after_hbm, *refs):
    del after_hbm
    outs_hbm, outs = refs[:2], refs[2:4]
    own, other, right, right_other, in_sem, write_sem = refs[4:]
    rows, columns = outs[0].shape
    wide = 256
    sources = ((own_hbm, at, own), (other_hbm, at, other), (right_hbm, block, right), (right_other_hbm, block, right_other))
    reads, writes = [], []
    for n, (source, begin, target) in enumerate(sources):
        reads.append(pltpu.make_async_copy(source.at[pl.ds(begin, target.shape[0])], target, in_sem.at[n]))
        reads[-1].start()
    for copy in reads:
        copy.wait()
    for k in range(columns // wide):
        cols = slice(wide * k, wide * k + wide)
        g = (nn(own[...], right[cols, :]) + nn(other[...], right_other[cols, :])).astype(BF16)
        outs[0][:, cols] = g[:rows]
        outs[1][:, cols] = g[rows:]
        if k % 2 == 1:
            cols = pl.ds(wide * (k - 1), 2 * wide)
            for n in range(2):
                copy = pltpu.make_async_copy(outs[n].at[:, cols], outs_hbm[n].at[:, cols], write_sem.at[k - 1 + n])
                copy.start()
                writes.append(copy)
    for copy in writes:
        copy.wait()


def params():
    return pltpu.CompilerParams(vmem_limit_bytes=VMEM_LIMIT)


VMEM = pl.BlockSpec(memory_space=pltpu.VMEM)
SMEM = pl.BlockSpec(memory_space=pltpu.SMEM)
ANY = pl.BlockSpec(memory_space=pl.ANY)


def cost(flops, moved):
    return pl.CostEstimate(flops=int(flops), bytes_accessed=int(moved), transcendentals=0)


def shape(dims, dtype=BF16):
    return jax.ShapeDtypeStruct(dims, dtype)


def swap(values):
    return lax.ppermute(values, "dp", [(i, i ^ 1) for i in range(32)])


def gradients(at, block, columns, own, other, right, right_other, after, name):
    rows, samples = own.shape[0] // 2, own.shape[1]
    piece = shape((rows // 2, columns))
    moved = (2 * rows * samples + 2 * samples * columns + rows * columns) * 2
    return pl.pallas_call(
        functools.partial(grad_kernel, at, block),
        out_shape=[piece] * 2,
        in_specs=[ANY] * 5,
        out_specs=[ANY] * 2,
        scratch_shapes=[pltpu.VMEM(piece.shape, BF16)] * 2
        + [pltpu.VMEM((rows, samples), BF16)] * 2
        + [pltpu.VMEM((columns, samples), BF16)] * 2
        + [pltpu.SemaphoreType.DMA((4,)), pltpu.SemaphoreType.DMA((columns // 256,))],
        compiler_params=params(),
        cost_estimate=cost(2 * rows * 2 * samples * columns, moved),
        name=name,
    )(own, other, right, right_other, after)


def reduce_send(step, send):
    return lax.ppermute(send, "dp", [(i, i ^ (PARTNERS[i & 1][step % 2] * SCALES[step])) for i in range(32)])


def reduce_add(step, keep, got):
    total = keep.astype(F32) + got.astype(F32)
    if step == 3:
        return total.astype(BF16), None
    half = total.shape[0] // 2
    return total[:half].astype(BF16), total[half:].astype(BF16)


def local(block_input, out_cotangent, w_in, w_out):
    samples, _, width = block_input.shape
    ff = w_out.shape[2]
    x = block_input[:, 0]
    cotangent = out_cotangent[:, 0]
    flat_in = w_in[0].reshape(width, 2 * ff)
    weight_out = w_out[0]
    packed_shape = shape((TOK, samples * 3 // 2, 128))
    index = lax.axis_index("dp").astype(jnp.int32).reshape(1)

    packed = pl.pallas_call(
        pack_kernel, out_shape=packed_shape, in_specs=[VMEM], out_specs=VMEM, compiler_params=params(),
        cost_estimate=cost(samples * width, 4 * samples * width), name="pack",
    )(x)
    recv = lax.all_to_all(packed, "token", split_axis=0, concat_axis=0, tiled=True)

    flat = shape((samples, width))
    own, send, inner, out_grad16 = pl.pallas_call(
        main_kernel,
        out_shape=[shape((width, samples)), shape((width + ff, samples)), shape((2 * ff, samples)), flat],
        in_specs=[SMEM, VMEM, VMEM, ANY, ANY, ANY],
        out_specs=[ANY] * 4,
        scratch_shapes=[
            pltpu.VMEM((width, 2 * ff), BF16),
            pltpu.VMEM((width, ff), BF16),
            pltpu.VMEM((samples, width), BF16),
            pltpu.VMEM((samples, width), BF16),
            pltpu.VMEM((samples, width), BF16),
            pltpu.VMEM((samples, ff), BF16),
            pltpu.VMEM((samples, width), F32),
            pltpu.VMEM((samples, ff), F32),
            pltpu.VMEM((samples, ff), F32),
            pltpu.VMEM((width, samples), BF16),
            pltpu.VMEM((width, samples), BF16),
            pltpu.VMEM((width + ff, samples), BF16),
            pltpu.VMEM((2 * ff, samples), BF16),
            pltpu.SemaphoreType.DMA((8,)),
            pltpu.SemaphoreType.DMA,
            pltpu.SemaphoreType.DMA,
            pltpu.SemaphoreType.DMA((14,)),
        ],
        compiler_params=params(),
        cost_estimate=cost(8 * samples * width * ff, 18e6),
        name="main",
    )(index, x, recv, cotangent, flat_in, weight_out)
    other, inner_other = swap(send), swap(inner)

    half = width // 2
    down = gradients(0, width, ff, own, other, send, other, inner, "down_grads")
    gate = gradients(half, 0, ff, own, other, inner, inner_other, down[1], "gate_grads")
    up = gradients(half, ff, ff, own, other, inner, inner_other, gate[1], "up_grads")
    kept = [grads[0] for grads in (down, gate, up)]
    got = [reduce_send(0, grads[1]) for grads in (down, gate, up)]

    pre_grad, back = pl.pallas_call(
        input_kernel,
        out_shape=[shape((samples, width), F32), packed_shape],
        in_specs=[VMEM, ANY, VMEM, VMEM, VMEM, ANY],
        out_specs=[VMEM] * 2,
        scratch_shapes=[
            pltpu.VMEM((width, 2 * ff), BF16),
            pltpu.VMEM((samples, 2 * ff), BF16),
            pltpu.VMEM((samples, width), F32),
            pltpu.SemaphoreType.DMA((width // 256,)),
        ],
        compiler_params=params(),
        cost_estimate=cost(4 * samples * width * ff, 14e6),
        name="input",
    )(inner, flat_in, x, recv, out_grad16, up[1])
    returned = lax.all_to_all(back, "token", split_axis=0, concat_axis=0, tiled=True)

    input_grad = pl.pallas_call(
        final_kernel, out_shape=flat, in_specs=[VMEM] * 2, out_specs=VMEM,
        compiler_params=params(), cost_estimate=cost(samples * width, 8 * samples * width), name="final",
    )(pre_grad, returned)

    previous = None
    for which, step in ((0, 0), (1, 0), (0, 1), (2, 0), (1, 1), (0, 2), (2, 1), (1, 2), (0, 3), (2, 2), (1, 3), (2, 3)):
        arrived = got[which]
        if previous is not None:
            arrived, previous = lax.optimization_barrier((arrived, previous))
        if (which, step) == (0, 3):
            arrived, input_grad = lax.optimization_barrier((arrived, input_grad))
        kept[which], sent = reduce_add(step, kept[which], arrived)
        previous = kept[which] if sent is None else sent
        if step < 3:
            got[which] = reduce_send(step + 1, sent)

    return (input_grad[:, None, :], jnp.stack(kept[1:], axis=1)[None], kept[0][None])


def solution(mesh):
    placed = (
        P("dp", "token", None),
        P("dp", "token", None),
        P("token", None, None, None),
        P("token", None, None),
    )
    return jax.shard_map(
        local,
        mesh=mesh,
        in_specs=placed,
        out_specs=(P("dp", "token", None), P("token", "dp", None, None), P("token", "dp", None)),
        check_vma=False,
    )
```

```python
import functools

import jax
import jax.numpy as jnp
from jax import lax
from jax.experimental import pallas as pl
from jax.experimental.pallas import tpu as pltpu
from jax.sharding import PartitionSpec as P

EPS = 1e-06
TOK = 8
F32 = jnp.float32
BF16 = jnp.bfloat16
VMEM_LIMIT = 56 * 1024 * 1024


def low_lanes(rows):
    return lax.broadcasted_iota(jnp.int32, (rows, 128), 1) < 64


def turn(values):
    return pltpu.roll(values, 64, 1)


def pack(read, packed_ref):
    samples = packed_ref.shape[1] * 2 // 3
    half = samples // 2
    low, low_half = low_lanes(samples), low_lanes(half)
    for pair in range(TOK // 2):
        first, middle, last = read(3 * pair), read(3 * pair + 1), read(3 * pair + 2)
        even, odd = packed_ref.at[2 * pair], packed_ref.at[2 * pair + 1]
        even[:samples] = first.astype(BF16)
        even[samples:] = jnp.where(low_half, middle[:half], turn(middle[half:])).astype(BF16)
        odd[:samples] = turn(jnp.where(low, last, middle)).astype(BF16)
        odd[samples:] = jnp.where(low_half, turn(last[:half]), last[half:]).astype(BF16)


def unpack(packed_ref, write):
    samples = packed_ref.shape[1] * 2 // 3
    low = low_lanes(samples)
    for pair in range(TOK // 2):
        even, odd = packed_ref.at[2 * pair], packed_ref.at[2 * pair + 1]
        turned = turn(odd[:samples].astype(F32))
        rest = even[samples:].astype(F32)
        rest = jnp.concatenate([rest, turn(rest)], axis=0)
        rest_odd = odd[samples:].astype(F32)
        rest_odd = jnp.concatenate([turn(rest_odd), rest_odd], axis=0)
        write(3 * pair, even[:samples].astype(F32))
        write(3 * pair + 1, jnp.where(low, rest, turned))
        write(3 * pair + 2, jnp.where(low, turned, rest_odd))


def tile(t):
    return slice(128 * t, 128 * t + 128)


def pack_kernel(x_ref, packed_ref):
    pack(lambda t: x_ref[:, tile(t)].astype(F32), packed_ref)


def nn(a, b):
    return lax.dot_general(a, b, (((1,), (0,)), ((), ())), preferred_element_type=F32)


def nt(a, b):
    return lax.dot_general(a, b, (((1,), (1,)), ((), ())), preferred_element_type=F32)


def norm_state(x_ref, recv_ref, normed_ref):
    samples, width = x_ref.shape
    sums = [jnp.zeros((samples, 128), F32)]

    def add_mixed(t, mixed):
        v = x_ref[:, tile(t)].astype(F32) + mixed
        normed_ref[:, tile(t)] = v
        sums[0] = sums[0] + v * v

    unpack(recv_ref, add_mixed)
    scale = lax.rsqrt(jnp.sum(sums[0], axis=1, keepdims=True) / width + EPS)
    for t in range(width // 128):
        normed_ref[:, tile(t)] = normed_ref[:, tile(t)] * scale
    return scale


def main_kernel(
    index_ref, x_ref, recv_ref, cot_hbm, w_in_hbm, w_out_hbm,
    own_hbm, send_hbm, inner_hbm, grad16_hbm,
    w_in, w_out, cot, state, grad16, hidden, values, slope, silu, turned, own, send, inner,
    in_sem, out_sem, cot_sem, write_sem,
):
    samples, width = x_ref.shape
    ff = w_out.shape[1]
    wide = 256
    steps = ff // wide
    half = width // 2
    writes = []

    def write(source, target, begin, rows):
        place = pl.ds(begin, rows)
        writes.append(pltpu.make_async_copy(source.at[place], target.at[place], write_sem.at[len(writes)]))
        writes[-1].start()

    def w_in_copy(j, c):
        cols = pl.ds(c * ff + j * wide, wide)
        return pltpu.make_async_copy(w_in_hbm.at[:, cols], w_in.at[:, cols], in_sem.at[2 * j + c])

    for j in range(steps):
        w_in_copy(j, 0).start()
        w_in_copy(j, 1).start()
    out_copy = pltpu.make_async_copy(w_out_hbm, w_out, out_sem)
    out_copy.start()
    cot_copy = pltpu.make_async_copy(cot_hbm, cot, cot_sem)
    cot_copy.start()

    rank = index_ref[0]

    def block(place, flavour):
        rx, rz = ((0, 3 - 2 * flavour, 1 + 2 * flavour, 2)[at] for at in divmod(place, 4))
        return 4 * rz + rx

    core = rank & 1

    def spread(at):
        for p in range(16):
            place = slice(at + 48 * p, at + 48 * p + 48)
            mine = (rank ^ (2 * block(p, core))) * 48
            theirs = (rank ^ (2 * block(p, 1 - core) + 1)) * 48
            own[place, :] = turned[pl.ds(pl.multiple_of(mine, 48), 48), :]
            send[place, :] = turned[pl.ds(pl.multiple_of(theirs, 48), 48), :]
        write(send, send_hbm, at, half)
        write(own, own_hbm, at, half)

    norm_state(x_ref, recv_ref, values)
    for t in range(width // 128):
        state[:, tile(t)] = values[:, tile(t)].astype(BF16)

    for j in range(steps):
        cols = slice(wide * j, wide * j + wide)
        w_in_copy(j, 0).wait()
        gate = nn(state[...], w_in[:, cols])
        w_in_copy(j, 1).wait()
        up = nn(state[...], w_in[:, ff + wide * j : ff + wide * j + wide])
        sigma = jax.nn.sigmoid(gate)
        silu_gate = gate * sigma
        part = (silu_gate * up).astype(BF16)
        hidden[:, cols] = part
        send[width + wide * j : width + wide * j + wide, :] = part
        silu[:, cols] = silu_gate
        slope[:, cols] = up * sigma * (1.0 + gate * (1.0 - sigma))
    write(send, send_hbm, width, ff)

    out_copy.wait()
    for d in range(width // wide):
        cols = slice(wide * d, wide * d + wide)
        values[:, cols] = nt(hidden[...], w_out[cols, :]) + state[:, cols].astype(F32)
    for t in range(width // 128):
        turned[tile(t), :] = state[:, tile(t)].T
    spread(half)
    cot_copy.wait()
    squares = jnp.zeros((samples, 128), F32)
    products = jnp.zeros((samples, 128), F32)
    for t in range(width // 128):
        v = values[:, tile(t)]
        squares = squares + v * v
        products = products + v * cot[:, tile(t)].astype(F32)
    scale = lax.rsqrt(jnp.sum(squares, axis=1, keepdims=True) / width + EPS)
    mean = scale * jnp.sum(products, axis=1, keepdims=True) / width
    for t in range(width // 128):
        out_normed = values[:, tile(t)] * scale
        g16 = (scale * (cot[:, tile(t)].astype(F32) - out_normed * mean)).astype(BF16)
        grad16[:, tile(t)] = g16
        turned[tile(t), :] = g16.T
    write(grad16, grad16_hbm, 0, samples)
    spread(0)
    for j in range(steps):
        cols = slice(wide * j, wide * j + wide)
        hidden_grad = nn(grad16[...], w_out[:, cols])
        inner[cols, :] = (hidden_grad * slope[:, cols]).astype(BF16)
        inner[ff + wide * j : ff + wide * j + wide, :] = (hidden_grad * silu[:, cols]).astype(BF16)
        write(inner, inner_hbm, wide * j, wide)
        write(inner, inner_hbm, ff + wide * j, wide)
    for copy in writes:
        copy.wait()


def input_kernel(
    inner_ref, w_in_hbm, x_ref, recv_ref, grad_ref, after_ref, pre_ref, packed_ref, w_in, inner, normed, sem
):
    del after_ref
    samples, width = x_ref.shape
    wide = 256

    def copy(d):
        rows = pl.ds(d * wide, wide)
        return pltpu.make_async_copy(w_in_hbm.at[rows], w_in.at[rows], sem.at[d])

    for d in range(width // wide):
        copy(d).start()
    scale = norm_state(x_ref, recv_ref, normed)
    for j in range(inner.shape[1] // samples):
        inner[:, samples * j : samples * j + samples] = inner_ref[samples * j : samples * j + samples, :]
    products = jnp.zeros((samples, 128), F32)
    for d in range(width // wide):
        copy(d).wait()
        cols = slice(wide * d, wide * d + wide)
        g = nt(inner[...], w_in[cols, :]) + grad_ref[:, cols].astype(F32)
        pre_ref[:, cols] = g
        p = g * normed[:, cols]
        products = products + p[:, :128] + p[:, 128:]
    mean = jnp.sum(products, axis=1, keepdims=True) / width
    for t in range(width // 128):
        pre_ref[:, tile(t)] = scale * (pre_ref[:, tile(t)] - normed[:, tile(t)] * mean)
    pack(lambda t: pre_ref[:, tile(t)], packed_ref)


def final_kernel(pre_ref, recv_ref, out_ref):
    def write(t, returned):
        out_ref[:, tile(t)] = (pre_ref[:, tile(t)] + returned).astype(BF16)

    unpack(recv_ref, write)


PARTNERS = ((1, 3), (3, 1))
X_FIRST, Z_FIRST = (2, 2, 8, 8), (8, 8, 2, 2)


def grad_kernel(x_first, at, block, own_hbm, other_hbm, right_hbm, right_other_hbm, after_hbm, *refs):
    del after_hbm
    outs_hbm, outs = refs[:2], refs[2:4]
    own, other, right, right_other, in_sem, write_sem = refs[4:]
    rows, columns = outs[0].shape
    wide = 256
    sources = ((own_hbm, at, own), (other_hbm, at, other), (right_hbm, block, right), (right_other_hbm, block, right_other))
    reads, writes = [], []
    for n, (source, begin, target) in enumerate(sources):
        reads.append(pltpu.make_async_copy(source.at[pl.ds(begin, target.shape[0])], target, in_sem.at[n]))
        reads[-1].start()
    for copy in reads:
        copy.wait()
    for k in range(columns // wide):
        cols = slice(wide * k, wide * k + wide)
        g = (nn(own[...], right[cols, :]) + nn(other[...], right_other[cols, :])).astype(BF16)
        if x_first:
            outs[0][:, cols] = g[:rows]
            outs[1][:, cols] = g[rows:]
        else:
            for p in range(16):
                half, to = divmod(4 * (p % 4) + p // 4, 8)
                outs[half][48 * to : 48 * to + 48, cols] = g[48 * p : 48 * p + 48]
        if k % 2 == 1 or k == columns // wide - 1:
            begin = k // 2 * 2
            cols = pl.ds(wide * begin, wide * (k + 1 - begin))
            for n in range(2):
                copy = pltpu.make_async_copy(outs[n].at[:, cols], outs_hbm[n].at[:, cols], write_sem.at[begin + n])
                copy.start()
                writes.append(copy)
    for copy in writes:
        copy.wait()


def params():
    return pltpu.CompilerParams(vmem_limit_bytes=VMEM_LIMIT)


VMEM = pl.BlockSpec(memory_space=pltpu.VMEM)
SMEM = pl.BlockSpec(memory_space=pltpu.SMEM)
ANY = pl.BlockSpec(memory_space=pl.ANY)


def cost(flops, moved):
    return pl.CostEstimate(flops=int(flops), bytes_accessed=int(moved), transcendentals=0)


def shape(dims, dtype=BF16):
    return jax.ShapeDtypeStruct(dims, dtype)


def swap(values):
    return lax.ppermute(values, "dp", [(i, i ^ 1) for i in range(32)])


def gradients(x_first, at, block, columns, own, other, right, right_other, after, name):
    rows, samples = own.shape[0] // 2, own.shape[1]
    piece = shape((rows // 2, columns))
    moved = (2 * rows * samples + 2 * samples * columns + rows * columns) * 2
    return pl.pallas_call(
        functools.partial(grad_kernel, x_first, at, block),
        out_shape=[piece] * 2,
        in_specs=[ANY] * 5,
        out_specs=[ANY] * 2,
        scratch_shapes=[pltpu.VMEM(piece.shape, BF16)] * 2
        + [pltpu.VMEM((rows, samples), BF16)] * 2
        + [pltpu.VMEM((columns, samples), BF16)] * 2
        + [pltpu.SemaphoreType.DMA((4,)), pltpu.SemaphoreType.DMA((columns // 256 + 1,))],
        compiler_params=params(),
        cost_estimate=cost(2 * rows * 2 * samples * columns, moved),
        name=name,
    )(own, other, right, right_other, after)


def reduce_send(scales, step, send):
    return lax.ppermute(send, "dp", [(i, i ^ (PARTNERS[i & 1][step % 2] * scales[step])) for i in range(32)])


def reduce_add(step, keep, got):
    total = keep.astype(F32) + got.astype(F32)
    if step == 3:
        return total.astype(BF16), None
    half = total.shape[0] // 2
    return total[:half].astype(BF16), total[half:].astype(BF16)


def local(block_input, out_cotangent, w_in, w_out):
    samples, _, width = block_input.shape
    ff = w_out.shape[2]
    x = block_input[:, 0]
    cotangent = out_cotangent[:, 0]
    flat_in = w_in[0].reshape(width, 2 * ff)
    weight_out = w_out[0]
    packed_shape = shape((TOK, samples * 3 // 2, 128))
    index = lax.axis_index("dp").astype(jnp.int32).reshape(1)

    packed = pl.pallas_call(
        pack_kernel, out_shape=packed_shape, in_specs=[VMEM], out_specs=VMEM, compiler_params=params(),
        cost_estimate=cost(samples * width, 4 * samples * width), name="pack",
    )(x)
    recv = lax.all_to_all(packed, "token", split_axis=0, concat_axis=0, tiled=True)

    flat = shape((samples, width))
    own, send, inner, out_grad16 = pl.pallas_call(
        main_kernel,
        out_shape=[shape((width, samples)), shape((width + ff, samples)), shape((2 * ff, samples)), flat],
        in_specs=[SMEM, VMEM, VMEM, ANY, ANY, ANY],
        out_specs=[ANY] * 4,
        scratch_shapes=[
            pltpu.VMEM((width, 2 * ff), BF16),
            pltpu.VMEM((width, ff), BF16),
            pltpu.VMEM((samples, width), BF16),
            pltpu.VMEM((samples, width), BF16),
            pltpu.VMEM((samples, width), BF16),
            pltpu.VMEM((samples, ff), BF16),
            pltpu.VMEM((samples, width), F32),
            pltpu.VMEM((samples, ff), F32),
            pltpu.VMEM((samples, ff), F32),
            pltpu.VMEM((width, samples), BF16),
            pltpu.VMEM((width, samples), BF16),
            pltpu.VMEM((width + ff, samples), BF16),
            pltpu.VMEM((2 * ff, samples), BF16),
            pltpu.SemaphoreType.DMA((8,)),
            pltpu.SemaphoreType.DMA,
            pltpu.SemaphoreType.DMA,
            pltpu.SemaphoreType.DMA((14,)),
        ],
        compiler_params=params(),
        cost_estimate=cost(8 * samples * width * ff, 18e6),
        name="main",
    )(index, x, recv, cotangent, flat_in, weight_out)
    other, inner_other = swap(send), swap(inner)

    half, split = width // 2, 768
    down = gradients(True, 0, width, ff, own, other, send, other, inner, "down_grads")
    low = gradients(False, half, 0, split, own, other, inner, inner_other, down[1], "low_grads")
    high = gradients(True, half, split, 2 * ff - split, own, other, inner, inner_other, low[1], "high_grads")
    orders = (X_FIRST, Z_FIRST, X_FIRST)
    kept = [grads[0] for grads in (down, low, high)]
    got = [reduce_send(order, 0, grads[1]) for order, grads in zip(orders, (down, low, high))]

    pre_grad, back = pl.pallas_call(
        input_kernel,
        out_shape=[shape((samples, width), F32), packed_shape],
        in_specs=[VMEM, ANY, VMEM, VMEM, VMEM, ANY],
        out_specs=[VMEM] * 2,
        scratch_shapes=[
            pltpu.VMEM((width, 2 * ff), BF16),
            pltpu.VMEM((samples, 2 * ff), BF16),
            pltpu.VMEM((samples, width), F32),
            pltpu.SemaphoreType.DMA((width // 256,)),
        ],
        compiler_params=params(),
        cost_estimate=cost(4 * samples * width * ff, 14e6),
        name="input",
    )(inner, flat_in, x, recv, out_grad16, high[1])
    returned = lax.all_to_all(back, "token", split_axis=0, concat_axis=0, tiled=True)

    input_grad = pl.pallas_call(
        final_kernel, out_shape=flat, in_specs=[VMEM] * 2, out_specs=VMEM,
        compiler_params=params(), cost_estimate=cost(samples * width, 8 * samples * width), name="final",
    )(pre_grad, returned)

    previous = None
    for which, step in ((0, 0), (1, 0), (2, 0), (0, 1), (2, 1), (0, 2), (1, 1), (2, 2), (1, 2), (0, 3), (1, 3), (2, 3)):
        arrived = got[which]
        if previous is not None:
            arrived, previous = lax.optimization_barrier((arrived, previous))
        if (which, step) == (2, 2):
            arrived, input_grad = lax.optimization_barrier((arrived, input_grad))
        kept[which], sent = reduce_add(step, kept[which], arrived)
        previous = kept[which] if sent is None else sent
        if step < 3:
            got[which] = reduce_send(orders[which], step + 1, sent)

    in_grad = jnp.concatenate(kept[1:], axis=1).reshape(width // 32, 2, ff)
    return (input_grad[:, None, :], in_grad[None], kept[0][None])


def solution(mesh):
    placed = (
        P("dp", "token", None),
        P("dp", "token", None),
        P("token", None, None, None),
        P("token", None, None),
    )
    return jax.shard_map(
        local,
        mesh=mesh,
        in_specs=placed,
        out_specs=(P("dp", "token", None), P("token", "dp", None, None), P("token", "dp", None)),
        check_vma=False,
    )
```

```python
import functools

import jax
import jax.numpy as jnp
from jax import lax
from jax.experimental import pallas as pl
from jax.experimental.pallas import tpu as pltpu
from jax.sharding import PartitionSpec as P

EPS = 1e-06
TOK = 8
F32 = jnp.float32
BF16 = jnp.bfloat16
VMEM_LIMIT = 56 * 1024 * 1024


def low_lanes(rows):
    return lax.broadcasted_iota(jnp.int32, (rows, 128), 1) < 64


def turn(values):
    return pltpu.roll(values, 64, 1)


def pack(read, packed_ref):
    samples = packed_ref.shape[1] * 2 // 3
    half = samples // 2
    low, low_half = low_lanes(samples), low_lanes(half)
    for pair in range(TOK // 2):
        first, middle, last = read(3 * pair), read(3 * pair + 1), read(3 * pair + 2)
        even, odd = packed_ref.at[2 * pair], packed_ref.at[2 * pair + 1]
        even[:samples] = first.astype(BF16)
        even[samples:] = jnp.where(low_half, middle[:half], turn(middle[half:])).astype(BF16)
        odd[:samples] = turn(jnp.where(low, last, middle)).astype(BF16)
        odd[samples:] = jnp.where(low_half, turn(last[:half]), last[half:]).astype(BF16)


def unpack(packed_ref, write):
    samples = packed_ref.shape[1] * 2 // 3
    low = low_lanes(samples)
    for pair in range(TOK // 2):
        even, odd = packed_ref.at[2 * pair], packed_ref.at[2 * pair + 1]
        turned = turn(odd[:samples].astype(F32))
        rest = even[samples:].astype(F32)
        rest = jnp.concatenate([rest, turn(rest)], axis=0)
        rest_odd = odd[samples:].astype(F32)
        rest_odd = jnp.concatenate([turn(rest_odd), rest_odd], axis=0)
        write(3 * pair, even[:samples].astype(F32))
        write(3 * pair + 1, jnp.where(low, rest, turned))
        write(3 * pair + 2, jnp.where(low, turned, rest_odd))


def tile(t):
    return slice(128 * t, 128 * t + 128)


def pack_kernel(x_ref, packed_ref):
    pack(lambda t: x_ref[:, tile(t)].astype(F32), packed_ref)


def nn(a, b):
    return lax.dot_general(a, b, (((1,), (0,)), ((), ())), preferred_element_type=F32)


def nt(a, b):
    return lax.dot_general(a, b, (((1,), (1,)), ((), ())), preferred_element_type=F32)


def norm_state(x_ref, recv_ref, normed_ref):
    samples, width = x_ref.shape
    sums = [jnp.zeros((samples, 128), F32)]

    def add_mixed(t, mixed):
        v = x_ref[:, tile(t)].astype(F32) + mixed
        normed_ref[:, tile(t)] = v
        sums[0] = sums[0] + v * v

    unpack(recv_ref, add_mixed)
    scale = lax.rsqrt(jnp.sum(sums[0], axis=1, keepdims=True) / width + EPS)
    for t in range(width // 128):
        normed_ref[:, tile(t)] = normed_ref[:, tile(t)] * scale
    return scale


def main_kernel(
    index_ref, x_ref, recv_ref, cot_hbm, w_in_hbm, w_out_hbm,
    own_hbm, send_hbm, inner_hbm, grad16_hbm,
    w_in, w_out, cot, state, grad16, hidden, values, slope, silu, turned, own, send, inner,
    in_sem, out_sem, cot_sem, write_sem,
):
    samples, width = x_ref.shape
    ff = w_out.shape[1]
    wide = 256
    steps = ff // wide
    half = width // 2
    writes = []

    def write(source, target, begin, rows):
        place = pl.ds(begin, rows)
        writes.append(pltpu.make_async_copy(source.at[place], target.at[place], write_sem.at[len(writes)]))
        writes[-1].start()

    def w_in_copy(j, c):
        cols = pl.ds(c * ff + j * wide, wide)
        return pltpu.make_async_copy(w_in_hbm.at[:, cols], w_in.at[:, cols], in_sem.at[2 * j + c])

    for j in range(steps):
        w_in_copy(j, 0).start()
        w_in_copy(j, 1).start()
    out_copy = pltpu.make_async_copy(w_out_hbm, w_out, out_sem)
    out_copy.start()
    cot_copy = pltpu.make_async_copy(cot_hbm, cot, cot_sem)
    cot_copy.start()

    rank = index_ref[0]

    def block(place, flavour):
        rx, rz = ((0, 3 - 2 * flavour, 1 + 2 * flavour, 2)[at] for at in divmod(place, 4))
        return 4 * rz + rx

    core = rank & 1

    def spread(at):
        for p in range(16):
            place = slice(at + 48 * p, at + 48 * p + 48)
            mine = (rank ^ (2 * block(p, core))) * 48
            theirs = (rank ^ (2 * block(p, 1 - core) + 1)) * 48
            own[place, :] = turned[pl.ds(pl.multiple_of(mine, 48), 48), :]
            send[place, :] = turned[pl.ds(pl.multiple_of(theirs, 48), 48), :]
        write(send, send_hbm, at, half)
        write(own, own_hbm, at, half)

    norm_state(x_ref, recv_ref, values)
    for t in range(width // 128):
        state[:, tile(t)] = values[:, tile(t)].astype(BF16)

    for j in range(steps):
        cols = slice(wide * j, wide * j + wide)
        w_in_copy(j, 0).wait()
        gate = nn(state[...], w_in[:, cols])
        w_in_copy(j, 1).wait()
        up = nn(state[...], w_in[:, ff + wide * j : ff + wide * j + wide])
        sigma = jax.nn.sigmoid(gate)
        silu_gate = gate * sigma
        part = (silu_gate * up).astype(BF16)
        hidden[:, cols] = part
        send[width + wide * j : width + wide * j + wide, :] = part
        silu[:, cols] = silu_gate
        slope[:, cols] = up * sigma * (1.0 + gate * (1.0 - sigma))
    write(send, send_hbm, width, ff)

    out_copy.wait()
    for d in range(width // wide):
        cols = slice(wide * d, wide * d + wide)
        values[:, cols] = nt(hidden[...], w_out[cols, :]) + state[:, cols].astype(F32)
    for t in range(width // 128):
        turned[tile(t), :] = state[:, tile(t)].T
    spread(half)
    cot_copy.wait()
    squares = jnp.zeros((samples, 128), F32)
    products = jnp.zeros((samples, 128), F32)
    for t in range(width // 128):
        v = values[:, tile(t)]
        squares = squares + v * v
        products = products + v * cot[:, tile(t)].astype(F32)
    scale = lax.rsqrt(jnp.sum(squares, axis=1, keepdims=True) / width + EPS)
    mean = scale * jnp.sum(products, axis=1, keepdims=True) / width
    for t in range(width // 128):
        out_normed = values[:, tile(t)] * scale
        g16 = (scale * (cot[:, tile(t)].astype(F32) - out_normed * mean)).astype(BF16)
        grad16[:, tile(t)] = g16
        turned[tile(t), :] = g16.T
    write(grad16, grad16_hbm, 0, samples)
    spread(0)
    for j in range(steps):
        cols = slice(wide * j, wide * j + wide)
        hidden_grad = nn(grad16[...], w_out[:, cols])
        inner[cols, :] = (hidden_grad * slope[:, cols]).astype(BF16)
        inner[ff + wide * j : ff + wide * j + wide, :] = (hidden_grad * silu[:, cols]).astype(BF16)
        write(inner, inner_hbm, wide * j, wide)
        write(inner, inner_hbm, ff + wide * j, wide)
    for copy in writes:
        copy.wait()


def input_kernel(
    inner_ref, w_in_hbm, x_ref, recv_ref, grad_ref, after_ref, pre_ref, packed_ref, w_in, inner, normed, sem
):
    del after_ref
    samples, width = x_ref.shape
    wide = 256

    def copy(d):
        rows = pl.ds(d * wide, wide)
        return pltpu.make_async_copy(w_in_hbm.at[rows], w_in.at[rows], sem.at[d])

    for d in range(width // wide):
        copy(d).start()
    scale = norm_state(x_ref, recv_ref, normed)
    for j in range(inner.shape[1] // samples):
        inner[:, samples * j : samples * j + samples] = inner_ref[samples * j : samples * j + samples, :]
    products = jnp.zeros((samples, 128), F32)
    for d in range(width // wide):
        copy(d).wait()
        cols = slice(wide * d, wide * d + wide)
        g = nt(inner[...], w_in[cols, :]) + grad_ref[:, cols].astype(F32)
        pre_ref[:, cols] = g
        p = g * normed[:, cols]
        products = products + p[:, :128] + p[:, 128:]
    mean = jnp.sum(products, axis=1, keepdims=True) / width
    for t in range(width // 128):
        pre_ref[:, tile(t)] = scale * (pre_ref[:, tile(t)] - normed[:, tile(t)] * mean)
    pack(lambda t: pre_ref[:, tile(t)], packed_ref)


def final_kernel(pre_ref, recv_ref, out_ref):
    def write(t, returned):
        out_ref[:, tile(t)] = (pre_ref[:, tile(t)] + returned).astype(BF16)

    unpack(recv_ref, write)


PARTNERS = ((1, 3), (3, 1))
X_FIRST, Z_FIRST = (2, 2, 8, 8), (8, 8, 2, 2)


def grad_kernel(x_first, at, block, own_hbm, other_hbm, right_hbm, right_other_hbm, after_hbm, *refs):
    del after_hbm
    outs_hbm, outs = refs[:2], refs[2:4]
    own, other, right, right_other, in_sem, write_sem = refs[4:]
    rows, columns = outs[0].shape
    wide = 256
    sources = ((own_hbm, at, own), (other_hbm, at, other), (right_hbm, block, right), (right_other_hbm, block, right_other))
    reads, writes = [], []
    for n, (source, begin, target) in enumerate(sources):
        reads.append(pltpu.make_async_copy(source.at[pl.ds(begin, target.shape[0])], target, in_sem.at[n]))
        reads[-1].start()
    for copy in reads:
        copy.wait()
    for k in range(columns // wide):
        cols = slice(wide * k, wide * k + wide)
        g = (nn(own[...], right[cols, :]) + nn(other[...], right_other[cols, :])).astype(BF16)
        if x_first:
            outs[0][:, cols] = g[:rows]
            outs[1][:, cols] = g[rows:]
        else:
            for p in range(16):
                half, to = divmod(4 * (p % 4) + p // 4, 8)
                outs[half][48 * to : 48 * to + 48, cols] = g[48 * p : 48 * p + 48]
        if k % 2 == 1 or k == columns // wide - 1:
            begin = k // 2 * 2
            cols = pl.ds(wide * begin, wide * (k + 1 - begin))
            for n in range(2):
                copy = pltpu.make_async_copy(outs[n].at[:, cols], outs_hbm[n].at[:, cols], write_sem.at[begin + n])
                copy.start()
                writes.append(copy)
    for copy in writes:
        copy.wait()


def params():
    return pltpu.CompilerParams(vmem_limit_bytes=VMEM_LIMIT)


VMEM = pl.BlockSpec(memory_space=pltpu.VMEM)
SMEM = pl.BlockSpec(memory_space=pltpu.SMEM)
ANY = pl.BlockSpec(memory_space=pl.ANY)


def cost(flops, moved):
    return pl.CostEstimate(flops=int(flops), bytes_accessed=int(moved), transcendentals=0)


def shape(dims, dtype=BF16):
    return jax.ShapeDtypeStruct(dims, dtype)


def swap(values):
    return lax.ppermute(values, "dp", [(i, i ^ 1) for i in range(32)])


def gradients(x_first, at, block, columns, own, other, right, right_other, after, name):
    rows, samples = own.shape[0] // 2, own.shape[1]
    piece = shape((rows // 2, columns))
    moved = (2 * rows * samples + 2 * samples * columns + rows * columns) * 2
    return pl.pallas_call(
        functools.partial(grad_kernel, x_first, at, block),
        out_shape=[piece] * 2,
        in_specs=[ANY] * 5,
        out_specs=[ANY] * 2,
        scratch_shapes=[pltpu.VMEM(piece.shape, BF16)] * 2
        + [pltpu.VMEM((rows, samples), BF16)] * 2
        + [pltpu.VMEM((columns, samples), BF16)] * 2
        + [pltpu.SemaphoreType.DMA((4,)), pltpu.SemaphoreType.DMA((columns // 256 + 1,))],
        compiler_params=params(),
        cost_estimate=cost(2 * rows * 2 * samples * columns, moved),
        name=name,
    )(own, other, right, right_other, after)


def reduce_send(scales, step, send):
    return lax.ppermute(send, "dp", [(i, i ^ (PARTNERS[i & 1][step % 2] * scales[step])) for i in range(32)])


def reduce_add(step, keep, got):
    total = keep.astype(F32) + got.astype(F32)
    if step == 3:
        return total.astype(BF16), None
    half = total.shape[0] // 2
    return total[:half].astype(BF16), total[half:].astype(BF16)


def local(block_input, out_cotangent, w_in, w_out):
    samples, _, width = block_input.shape
    ff = w_out.shape[2]
    x = block_input[:, 0]
    cotangent = out_cotangent[:, 0]
    flat_in = w_in[0].reshape(width, 2 * ff)
    weight_out = w_out[0]
    packed_shape = shape((TOK, samples * 3 // 2, 128))
    index = lax.axis_index("dp").astype(jnp.int32).reshape(1)

    packed = pl.pallas_call(
        pack_kernel, out_shape=packed_shape, in_specs=[VMEM], out_specs=VMEM, compiler_params=params(),
        cost_estimate=cost(samples * width, 4 * samples * width), name="pack",
    )(x)
    recv = lax.all_to_all(packed, "token", split_axis=0, concat_axis=0, tiled=True)

    flat = shape((samples, width))
    own, send, inner, out_grad16 = pl.pallas_call(
        main_kernel,
        out_shape=[shape((width, samples)), shape((width + ff, samples)), shape((2 * ff, samples)), flat],
        in_specs=[SMEM, VMEM, VMEM, ANY, ANY, ANY],
        out_specs=[ANY] * 4,
        scratch_shapes=[
            pltpu.VMEM((width, 2 * ff), BF16),
            pltpu.VMEM((width, ff), BF16),
            pltpu.VMEM((samples, width), BF16),
            pltpu.VMEM((samples, width), BF16),
            pltpu.VMEM((samples, width), BF16),
            pltpu.VMEM((samples, ff), BF16),
            pltpu.VMEM((samples, width), F32),
            pltpu.VMEM((samples, ff), F32),
            pltpu.VMEM((samples, ff), F32),
            pltpu.VMEM((width, samples), BF16),
            pltpu.VMEM((width, samples), BF16),
            pltpu.VMEM((width + ff, samples), BF16),
            pltpu.VMEM((2 * ff, samples), BF16),
            pltpu.SemaphoreType.DMA((8,)),
            pltpu.SemaphoreType.DMA,
            pltpu.SemaphoreType.DMA,
            pltpu.SemaphoreType.DMA((14,)),
        ],
        compiler_params=params(),
        cost_estimate=cost(8 * samples * width * ff, 18e6),
        name="main",
    )(index, x, recv, cotangent, flat_in, weight_out)
    other, inner_other = swap(send), swap(inner)

    half, split = width // 2, 768
    down = gradients(False, 0, width, ff, own, other, send, other, inner, "down_grads")
    low = gradients(True, half, 0, split, own, other, inner, inner_other, down[1], "low_grads")
    high = gradients(True, half, split, 2 * ff - split, own, other, inner, inner_other, low[1], "high_grads")
    orders = (Z_FIRST, X_FIRST, X_FIRST)
    kept = [grads[0] for grads in (down, low, high)]
    got = [reduce_send(order, 0, grads[1]) for order, grads in zip(orders, (down, low, high))]

    pre_grad, back = pl.pallas_call(
        input_kernel,
        out_shape=[shape((samples, width), F32), packed_shape],
        in_specs=[VMEM, ANY, VMEM, VMEM, VMEM, ANY],
        out_specs=[VMEM] * 2,
        scratch_shapes=[
            pltpu.VMEM((width, 2 * ff), BF16),
            pltpu.VMEM((samples, 2 * ff), BF16),
            pltpu.VMEM((samples, width), F32),
            pltpu.SemaphoreType.DMA((width // 256,)),
        ],
        compiler_params=params(),
        cost_estimate=cost(4 * samples * width * ff, 14e6),
        name="input",
    )(inner, flat_in, x, recv, out_grad16, high[1])
    returned = lax.all_to_all(back, "token", split_axis=0, concat_axis=0, tiled=True)

    input_grad = pl.pallas_call(
        final_kernel, out_shape=flat, in_specs=[VMEM] * 2, out_specs=VMEM,
        compiler_params=params(), cost_estimate=cost(samples * width, 8 * samples * width), name="final",
    )(pre_grad, returned)

    previous = None
    for which, step in ((0, 0), (1, 0), (2, 0), (1, 1), (2, 1), (0, 1), (1, 2), (0, 2), (2, 2), (1, 3), (0, 3), (2, 3)):
        arrived = got[which]
        if previous is not None:
            arrived, previous = lax.optimization_barrier((arrived, previous))
        if (which, step) == (2, 2):
            arrived, input_grad = lax.optimization_barrier((arrived, input_grad))
        kept[which], sent = reduce_add(step, kept[which], arrived)
        previous = kept[which] if sent is None else sent
        if step < 3:
            got[which] = reduce_send(orders[which], step + 1, sent)

    in_grad = jnp.concatenate(kept[1:], axis=1).reshape(width // 32, 2, ff)
    return (input_grad[:, None, :], in_grad[None], kept[0][None])


def solution(mesh):
    placed = (
        P("dp", "token", None),
        P("dp", "token", None),
        P("token", None, None, None),
        P("token", None, None),
    )
    return jax.shard_map(
        local,
        mesh=mesh,
        in_specs=placed,
        out_specs=(P("dp", "token", None), P("token", "dp", None, None), P("token", "dp", None)),
        check_vma=False,
    )
```

```python
import functools

import jax
import jax.numpy as jnp
from jax import lax
from jax.experimental import pallas as pl
from jax.experimental.pallas import tpu as pltpu
from jax.sharding import PartitionSpec as P

EPS = 1e-06
TOK = 8
F32 = jnp.float32
BF16 = jnp.bfloat16
VMEM_LIMIT = 56 * 1024 * 1024


def low_lanes(rows):
    return lax.broadcasted_iota(jnp.int32, (rows, 128), 1) < 64


def turn(values):
    return pltpu.roll(values, 64, 1)


def pack(read, packed_ref):
    samples = packed_ref.shape[1] * 2 // 3
    half = samples // 2
    low, low_half = low_lanes(samples), low_lanes(half)
    for pair in range(TOK // 2):
        first, middle, last = read(3 * pair), read(3 * pair + 1), read(3 * pair + 2)
        even, odd = packed_ref.at[2 * pair], packed_ref.at[2 * pair + 1]
        even[:samples] = first.astype(BF16)
        even[samples:] = jnp.where(low_half, middle[:half], turn(middle[half:])).astype(BF16)
        odd[:samples] = turn(jnp.where(low, last, middle)).astype(BF16)
        odd[samples:] = jnp.where(low_half, turn(last[:half]), last[half:]).astype(BF16)


def unpack(packed_ref, write):
    samples = packed_ref.shape[1] * 2 // 3
    low = low_lanes(samples)
    for pair in range(TOK // 2):
        even, odd = packed_ref.at[2 * pair], packed_ref.at[2 * pair + 1]
        turned = turn(odd[:samples].astype(F32))
        rest = even[samples:].astype(F32)
        rest = jnp.concatenate([rest, turn(rest)], axis=0)
        rest_odd = odd[samples:].astype(F32)
        rest_odd = jnp.concatenate([turn(rest_odd), rest_odd], axis=0)
        write(3 * pair, even[:samples].astype(F32))
        write(3 * pair + 1, jnp.where(low, rest, turned))
        write(3 * pair + 2, jnp.where(low, turned, rest_odd))


def tile(t):
    return slice(128 * t, 128 * t + 128)


def pack_kernel(x_ref, packed_ref):
    pack(lambda t: x_ref[:, tile(t)].astype(F32), packed_ref)


def nn(a, b):
    return lax.dot_general(a, b, (((1,), (0,)), ((), ())), preferred_element_type=F32)


def nt(a, b):
    return lax.dot_general(a, b, (((1,), (1,)), ((), ())), preferred_element_type=F32)


def norm_state(x_ref, recv_ref, normed_ref):
    samples, width = x_ref.shape
    sums = [jnp.zeros((samples, 128), F32)]

    def add_mixed(t, mixed):
        v = x_ref[:, tile(t)].astype(F32) + mixed
        normed_ref[:, tile(t)] = v
        sums[0] = sums[0] + v * v

    unpack(recv_ref, add_mixed)
    scale = lax.rsqrt(jnp.sum(sums[0], axis=1, keepdims=True) / width + EPS)
    for t in range(width // 128):
        normed_ref[:, tile(t)] = normed_ref[:, tile(t)] * scale
    return scale


def main_kernel(
    index_ref, x_ref, recv_ref, cot_hbm, w_in_hbm, w_out_hbm,
    own_hbm, send_hbm, inner_hbm, grad16_hbm, w_in,
    w_out, cot, state, grad16, hidden, values, slope, silu, turned, own, send, inner,
    in_sem, out_sem, cot_sem, write_sem,
):
    samples, width = x_ref.shape
    ff = w_out.shape[1]
    wide = 256
    steps = ff // wide
    half = width // 2
    writes = []

    def write(source, target, begin, rows):
        place = pl.ds(begin, rows)
        writes.append(pltpu.make_async_copy(source.at[place], target.at[place], write_sem.at[len(writes)]))
        writes[-1].start()

    def w_in_copy(j, c):
        cols = pl.ds(c * ff + j * wide, wide)
        return pltpu.make_async_copy(w_in_hbm.at[:, cols], w_in.at[:, cols], in_sem.at[2 * j + c])

    for j in range(steps):
        w_in_copy(j, 0).start()
        w_in_copy(j, 1).start()
    out_copy = pltpu.make_async_copy(w_out_hbm, w_out, out_sem)
    out_copy.start()
    cot_copy = pltpu.make_async_copy(cot_hbm, cot, cot_sem)
    cot_copy.start()

    rank = index_ref[0]

    def block(place, flavour):
        rx, rz = ((0, 3 - 2 * flavour, 1 + 2 * flavour, 2)[at] for at in divmod(place, 4))
        return 4 * rz + rx

    core = rank & 1

    def spread(at):
        for p in range(16):
            place = slice(at + 48 * p, at + 48 * p + 48)
            mine = (rank ^ (2 * block(p, core))) * 48
            theirs = (rank ^ (2 * block(p, 1 - core) + 1)) * 48
            own[place, :] = turned[pl.ds(pl.multiple_of(mine, 48), 48), :]
            send[place, :] = turned[pl.ds(pl.multiple_of(theirs, 48), 48), :]
        write(send, send_hbm, at, half)
        write(own, own_hbm, at, half)

    norm_state(x_ref, recv_ref, values)
    for t in range(width // 128):
        state[:, tile(t)] = values[:, tile(t)].astype(BF16)

    for j in range(steps):
        cols = slice(wide * j, wide * j + wide)
        w_in_copy(j, 0).wait()
        gate = nn(state[...], w_in[:, cols])
        w_in_copy(j, 1).wait()
        up = nn(state[...], w_in[:, ff + wide * j : ff + wide * j + wide])
        sigma = jax.nn.sigmoid(gate)
        silu_gate = gate * sigma
        part = (silu_gate * up).astype(BF16)
        hidden[:, cols] = part
        send[width + wide * j : width + wide * j + wide, :] = part
        silu[:, cols] = silu_gate
        slope[:, cols] = up * sigma * (1.0 + gate * (1.0 - sigma))
    write(send, send_hbm, width, ff)

    out_copy.wait()
    for d in range(width // wide):
        cols = slice(wide * d, wide * d + wide)
        values[:, cols] = nt(hidden[...], w_out[cols, :]) + state[:, cols].astype(F32)
    for t in range(width // 128):
        turned[tile(t), :] = state[:, tile(t)].T
    spread(half)
    cot_copy.wait()
    squares = jnp.zeros((samples, 128), F32)
    products = jnp.zeros((samples, 128), F32)
    for t in range(width // 128):
        v = values[:, tile(t)]
        squares = squares + v * v
        products = products + v * cot[:, tile(t)].astype(F32)
    scale = lax.rsqrt(jnp.sum(squares, axis=1, keepdims=True) / width + EPS)
    mean = scale * jnp.sum(products, axis=1, keepdims=True) / width
    for t in range(width // 128):
        out_normed = values[:, tile(t)] * scale
        g16 = (scale * (cot[:, tile(t)].astype(F32) - out_normed * mean)).astype(BF16)
        grad16[:, tile(t)] = g16
        turned[tile(t), :] = g16.T
    write(grad16, grad16_hbm, 0, samples)
    spread(0)
    for j in range(steps):
        cols = slice(wide * j, wide * j + wide)
        hidden_grad = nn(grad16[...], w_out[:, cols])
        inner[cols, :] = (hidden_grad * slope[:, cols]).astype(BF16)
        inner[ff + wide * j : ff + wide * j + wide, :] = (hidden_grad * silu[:, cols]).astype(BF16)
        write(inner, inner_hbm, wide * j, wide)
        write(inner, inner_hbm, ff + wide * j, wide)
    for copy in writes:
        copy.wait()


def input_kernel(
    inner_ref, w_in, x_ref, recv_ref, grad_ref, after_ref, pre_ref, packed_ref, inner, normed
):
    del after_ref
    samples, width = x_ref.shape
    wide = 256

    scale = norm_state(x_ref, recv_ref, normed)
    for j in range(inner.shape[1] // samples):
        inner[:, samples * j : samples * j + samples] = inner_ref[samples * j : samples * j + samples, :]
    products = jnp.zeros((samples, 128), F32)
    for d in range(width // wide):
        cols = slice(wide * d, wide * d + wide)
        g = nt(inner[...], w_in[cols, :]) + grad_ref[:, cols].astype(F32)
        pre_ref[:, cols] = g
        p = g * normed[:, cols]
        products = products + p[:, :128] + p[:, 128:]
    mean = jnp.sum(products, axis=1, keepdims=True) / width
    for t in range(width // 128):
        pre_ref[:, tile(t)] = scale * (pre_ref[:, tile(t)] - normed[:, tile(t)] * mean)
    pack(lambda t: pre_ref[:, tile(t)], packed_ref)


def final_kernel(pre_ref, recv_ref, out_ref):
    def write(t, returned):
        out_ref[:, tile(t)] = (pre_ref[:, tile(t)] + returned).astype(BF16)

    unpack(recv_ref, write)


PARTNERS = ((1, 3), (3, 1))
X_FIRST, Z_FIRST = (2, 2, 8, 8), (8, 8, 2, 2)


def grad_kernel(x_first, at, block, own_hbm, other_hbm, right_hbm, right_other_hbm, after_hbm, *refs):
    del after_hbm
    outs_hbm, outs = refs[:2], refs[2:4]
    own, other, right, right_other, in_sem, write_sem = refs[4:]
    rows, columns = outs[0].shape
    wide = 256
    sources = ((own_hbm, at, own), (other_hbm, at, other), (right_hbm, block, right), (right_other_hbm, block, right_other))
    reads, writes = [], []
    for n, (source, begin, target) in enumerate(sources):
        reads.append(pltpu.make_async_copy(source.at[pl.ds(begin, target.shape[0])], target, in_sem.at[n]))
        reads[-1].start()
    for copy in reads:
        copy.wait()
    for k in range(columns // wide):
        cols = slice(wide * k, wide * k + wide)
        g = (nn(own[...], right[cols, :]) + nn(other[...], right_other[cols, :])).astype(BF16)
        if x_first:
            outs[0][:, cols] = g[:rows]
            outs[1][:, cols] = g[rows:]
        else:
            for p in range(16):
                half, to = divmod(4 * (p % 4) + p // 4, 8)
                outs[half][48 * to : 48 * to + 48, cols] = g[48 * p : 48 * p + 48]
        if k % 2 == 1 or k == columns // wide - 1:
            begin = k // 2 * 2
            cols = pl.ds(wide * begin, wide * (k + 1 - begin))
            for n in range(2):
                copy = pltpu.make_async_copy(outs[n].at[:, cols], outs_hbm[n].at[:, cols], write_sem.at[begin + n])
                copy.start()
                writes.append(copy)
    for copy in writes:
        copy.wait()


def params():
    return pltpu.CompilerParams(vmem_limit_bytes=VMEM_LIMIT)


VMEM = pl.BlockSpec(memory_space=pltpu.VMEM)
SMEM = pl.BlockSpec(memory_space=pltpu.SMEM)
ANY = pl.BlockSpec(memory_space=pl.ANY)


def cost(flops, moved):
    return pl.CostEstimate(flops=int(flops), bytes_accessed=int(moved), transcendentals=0)


def shape(dims, dtype=BF16):
    return jax.ShapeDtypeStruct(dims, dtype)


def swap(values):
    return lax.ppermute(values, "dp", [(i, i ^ 1) for i in range(32)])


def gradients(x_first, at, block, columns, own, other, right, right_other, after, name):
    rows, samples = own.shape[0] // 2, own.shape[1]
    piece = shape((rows // 2, columns))
    moved = (2 * rows * samples + 2 * samples * columns + rows * columns) * 2
    return pl.pallas_call(
        functools.partial(grad_kernel, x_first, at, block),
        out_shape=[piece] * 2,
        in_specs=[ANY] * 5,
        out_specs=[ANY] * 2,
        scratch_shapes=[pltpu.VMEM(piece.shape, BF16)] * 2
        + [pltpu.VMEM((rows, samples), BF16)] * 2
        + [pltpu.VMEM((columns, samples), BF16)] * 2
        + [pltpu.SemaphoreType.DMA((4,)), pltpu.SemaphoreType.DMA((columns // 256 + 1,))],
        compiler_params=params(),
        cost_estimate=cost(2 * rows * 2 * samples * columns, moved),
        name=name,
    )(own, other, right, right_other, after)


def reduce_send(scales, step, send):
    return lax.ppermute(send, "dp", [(i, i ^ (PARTNERS[i & 1][step % 2] * scales[step])) for i in range(32)])


def reduce_add(step, keep, got):
    total = keep.astype(F32) + got.astype(F32)
    if step == 3:
        return total.astype(BF16), None
    half = total.shape[0] // 2
    return total[:half].astype(BF16), total[half:].astype(BF16)


def local(block_input, out_cotangent, w_in, w_out):
    samples, _, width = block_input.shape
    ff = w_out.shape[2]
    x = block_input[:, 0]
    cotangent = out_cotangent[:, 0]
    flat_in = w_in[0].reshape(width, 2 * ff)
    weight_out = w_out[0]
    packed_shape = shape((TOK, samples * 3 // 2, 128))
    index = lax.axis_index("dp").astype(jnp.int32).reshape(1)

    packed = pl.pallas_call(
        pack_kernel, out_shape=packed_shape, in_specs=[VMEM], out_specs=VMEM, compiler_params=params(),
        cost_estimate=cost(samples * width, 4 * samples * width), name="pack",
    )(x)
    recv = lax.all_to_all(packed, "token", split_axis=0, concat_axis=0, tiled=True)

    flat = shape((samples, width))
    own, send, inner, out_grad16, held_in = pl.pallas_call(
        main_kernel,
        out_shape=[shape((width, samples)), shape((width + ff, samples)), shape((2 * ff, samples)), flat, pltpu.VMEM((width, 2 * ff), BF16)],
        in_specs=[SMEM, VMEM, VMEM, ANY, ANY, ANY],
        out_specs=[ANY] * 4 + [VMEM],
        scratch_shapes=[
            pltpu.VMEM((width, ff), BF16),
            pltpu.VMEM((samples, width), BF16),
            pltpu.VMEM((samples, width), BF16),
            pltpu.VMEM((samples, width), BF16),
            pltpu.VMEM((samples, ff), BF16),
            pltpu.VMEM((samples, width), F32),
            pltpu.VMEM((samples, ff), F32),
            pltpu.VMEM((samples, ff), F32),
            pltpu.VMEM((width, samples), BF16),
            pltpu.VMEM((width, samples), BF16),
            pltpu.VMEM((width + ff, samples), BF16),
            pltpu.VMEM((2 * ff, samples), BF16),
            pltpu.SemaphoreType.DMA((8,)),
            pltpu.SemaphoreType.DMA,
            pltpu.SemaphoreType.DMA,
            pltpu.SemaphoreType.DMA((14,)),
        ],
        compiler_params=params(),
        cost_estimate=cost(8 * samples * width * ff, 18e6),
        name="main",
    )(index, x, recv, cotangent, flat_in, weight_out)
    other, inner_other = swap(send), swap(inner)

    half, split = width // 2, 768
    down = gradients(True, 0, width, ff, own, other, send, other, inner, "down_grads")
    low = gradients(False, half, 0, split, own, other, inner, inner_other, down[1], "low_grads")
    high = gradients(True, half, split, 2 * ff - split, own, other, inner, inner_other, low[1], "high_grads")
    orders = (X_FIRST, Z_FIRST, X_FIRST)
    kept = [grads[0] for grads in (down, low, high)]
    got = [reduce_send(order, 0, grads[1]) for order, grads in zip(orders, (down, low, high))]

    pre_grad, back = pl.pallas_call(
        input_kernel,
        out_shape=[shape((samples, width), F32), packed_shape],
        in_specs=[VMEM] * 5 + [ANY],
        out_specs=[VMEM] * 2,
        scratch_shapes=[
            pltpu.VMEM((samples, 2 * ff), BF16),
            pltpu.VMEM((samples, width), F32),
        ],
        compiler_params=params(),
        cost_estimate=cost(4 * samples * width * ff, 14e6),
        name="input",
    )(inner, pltpu.with_memory_space_constraint(held_in, pltpu.VMEM), x, recv, out_grad16, high[1])
    returned = lax.all_to_all(back, "token", split_axis=0, concat_axis=0, tiled=True)

    input_grad = pl.pallas_call(
        final_kernel, out_shape=flat, in_specs=[VMEM] * 2, out_specs=VMEM,
        compiler_params=params(), cost_estimate=cost(samples * width, 8 * samples * width), name="final",
    )(pre_grad, returned)

    previous = None
    for which, step in ((0, 0), (1, 0), (2, 0), (0, 1), (2, 1), (0, 2), (1, 1), (2, 2), (1, 2), (0, 3), (1, 3), (2, 3)):
        arrived = got[which]
        if previous is not None:
            arrived, previous = lax.optimization_barrier((arrived, previous))
        if (which, step) == (2, 2):
            arrived, input_grad = lax.optimization_barrier((arrived, input_grad))
        kept[which], sent = reduce_add(step, kept[which], arrived)
        previous = kept[which] if sent is None else sent
        if step < 3:
            got[which] = reduce_send(orders[which], step + 1, sent)

    in_grad = jnp.concatenate(kept[1:], axis=1).reshape(width // 32, 2, ff)
    return (input_grad[:, None, :], in_grad[None], kept[0][None])


def solution(mesh):
    placed = (
        P("dp", "token", None),
        P("dp", "token", None),
        P("token", None, None, None),
        P("token", None, None),
    )
    return jax.shard_map(
        local,
        mesh=mesh,
        in_specs=placed,
        out_specs=(P("dp", "token", None), P("token", "dp", None, None), P("token", "dp", None)),
        check_vma=False,
    )
```

```python
import functools

import jax
import jax.numpy as jnp
from jax import lax
from jax.experimental import pallas as pl
from jax.experimental.pallas import tpu as pltpu
from jax.sharding import PartitionSpec as P

EPS = 1e-06
TOK = 8
F32 = jnp.float32
BF16 = jnp.bfloat16
VMEM_LIMIT = 56 * 1024 * 1024


def low_lanes(rows):
    return lax.broadcasted_iota(jnp.int32, (rows, 128), 1) < 64


def turn(values):
    return pltpu.roll(values, 64, 1)


def pack(read, packed_ref):
    samples = packed_ref.shape[1] * 2 // 3
    half = samples // 2
    low, low_half = low_lanes(samples), low_lanes(half)
    for pair in range(TOK // 2):
        first, middle, last = read(3 * pair), read(3 * pair + 1), read(3 * pair + 2)
        even, odd = packed_ref.at[2 * pair], packed_ref.at[2 * pair + 1]
        even[:samples] = first.astype(BF16)
        even[samples:] = jnp.where(low_half, middle[:half], turn(middle[half:])).astype(BF16)
        odd[:samples] = turn(jnp.where(low, last, middle)).astype(BF16)
        odd[samples:] = jnp.where(low_half, turn(last[:half]), last[half:]).astype(BF16)


def unpack(packed_ref, write):
    samples = packed_ref.shape[1] * 2 // 3
    low = low_lanes(samples)
    for pair in range(TOK // 2):
        even, odd = packed_ref.at[2 * pair], packed_ref.at[2 * pair + 1]
        turned = turn(odd[:samples].astype(F32))
        rest = even[samples:].astype(F32)
        rest = jnp.concatenate([rest, turn(rest)], axis=0)
        rest_odd = odd[samples:].astype(F32)
        rest_odd = jnp.concatenate([turn(rest_odd), rest_odd], axis=0)
        write(3 * pair, even[:samples].astype(F32))
        write(3 * pair + 1, jnp.where(low, rest, turned))
        write(3 * pair + 2, jnp.where(low, turned, rest_odd))


def tile(t):
    return slice(128 * t, 128 * t + 128)


def pack_kernel(x_ref, packed_ref):
    pack(lambda t: x_ref[:, tile(t)].astype(F32), packed_ref)


def nn(a, b):
    return lax.dot_general(a, b, (((1,), (0,)), ((), ())), preferred_element_type=F32)


def nt(a, b):
    return lax.dot_general(a, b, (((1,), (1,)), ((), ())), preferred_element_type=F32)


def norm_state(x_ref, recv_ref, normed_ref):
    samples, width = x_ref.shape
    sums = [jnp.zeros((samples, 128), F32)]

    def add_mixed(t, mixed):
        v = x_ref[:, tile(t)].astype(F32) + mixed
        normed_ref[:, tile(t)] = v
        sums[0] = sums[0] + v * v

    unpack(recv_ref, add_mixed)
    scale = lax.rsqrt(jnp.sum(sums[0], axis=1, keepdims=True) / width + EPS)
    for t in range(width // 128):
        normed_ref[:, tile(t)] = normed_ref[:, tile(t)] * scale
    return scale


def main_kernel(
    index_ref, x_ref, recv_ref, cot_hbm, w_in_hbm, w_out_hbm,
    own_hbm, send_hbm, inner_hbm, grad16_hbm, w_in,
    w_out, cot, state, grad16, hidden, values, slope, silu, turned, own, send, inner,
    in_sem, out_sem, cot_sem, write_sem,
):
    samples, width = x_ref.shape
    ff = w_out.shape[1]
    wide = 256
    steps = ff // wide
    half = width // 2
    writes = []

    def write(source, target, begin, rows):
        place = pl.ds(begin, rows)
        writes.append(pltpu.make_async_copy(source.at[place], target.at[place], write_sem.at[len(writes)]))
        writes[-1].start()

    def w_in_copy(j, c):
        cols = pl.ds(c * ff + j * wide, wide)
        return pltpu.make_async_copy(w_in_hbm.at[:, cols], w_in.at[:, cols], in_sem.at[2 * j + c])

    for j in range(steps):
        w_in_copy(j, 0).start()
        w_in_copy(j, 1).start()
    out_copy = pltpu.make_async_copy(w_out_hbm, w_out, out_sem)
    out_copy.start()
    cot_copy = pltpu.make_async_copy(cot_hbm, cot, cot_sem)
    cot_copy.start()

    rank = index_ref[0]

    def block(place, flavour):
        rx, rz = ((0, 3 - 2 * flavour, 1 + 2 * flavour, 2)[at] for at in divmod(place, 4))
        return 4 * rz + rx

    core = rank & 1

    def spread(at):
        for p in range(16):
            place = slice(at + 48 * p, at + 48 * p + 48)
            mine = (rank ^ (2 * block(p, core))) * 48
            theirs = (rank ^ (2 * block(p, 1 - core) + 1)) * 48
            own[place, :] = turned[pl.ds(pl.multiple_of(mine, 48), 48), :]
            send[place, :] = turned[pl.ds(pl.multiple_of(theirs, 48), 48), :]
        write(send, send_hbm, at, half)
        write(own, own_hbm, at, half)

    norm_state(x_ref, recv_ref, values)
    for t in range(width // 128):
        state[:, tile(t)] = values[:, tile(t)].astype(BF16)

    for j in range(steps):
        cols = slice(wide * j, wide * j + wide)
        w_in_copy(j, 0).wait()
        gate = nn(state[...], w_in[:, cols])
        w_in_copy(j, 1).wait()
        up = nn(state[...], w_in[:, ff + wide * j : ff + wide * j + wide])
        sigma = jax.nn.sigmoid(gate)
        silu_gate = gate * sigma
        part = (silu_gate * up).astype(BF16)
        hidden[:, cols] = part
        send[width + wide * j : width + wide * j + wide, :] = part
        silu[:, cols] = silu_gate
        slope[:, cols] = up * sigma * (1.0 + gate * (1.0 - sigma))
    write(send, send_hbm, width, ff)

    out_copy.wait()
    for d in range(width // wide):
        cols = slice(wide * d, wide * d + wide)
        values[:, cols] = nt(hidden[...], w_out[cols, :]) + state[:, cols].astype(F32)
    for t in range(width // 128):
        turned[tile(t), :] = state[:, tile(t)].T
    spread(half)
    cot_copy.wait()
    squares = jnp.zeros((samples, 128), F32)
    products = jnp.zeros((samples, 128), F32)
    for t in range(width // 128):
        v = values[:, tile(t)]
        squares = squares + v * v
        products = products + v * cot[:, tile(t)].astype(F32)
    scale = lax.rsqrt(jnp.sum(squares, axis=1, keepdims=True) / width + EPS)
    mean = scale * jnp.sum(products, axis=1, keepdims=True) / width
    for t in range(width // 128):
        out_normed = values[:, tile(t)] * scale
        g16 = (scale * (cot[:, tile(t)].astype(F32) - out_normed * mean)).astype(BF16)
        grad16[:, tile(t)] = g16
        turned[tile(t), :] = g16.T
    write(grad16, grad16_hbm, 0, samples)
    spread(0)
    for j in range(steps):
        cols = slice(wide * j, wide * j + wide)
        hidden_grad = nn(grad16[...], w_out[:, cols])
        inner[cols, :] = (hidden_grad * slope[:, cols]).astype(BF16)
        inner[ff + wide * j : ff + wide * j + wide, :] = (hidden_grad * silu[:, cols]).astype(BF16)
        write(inner, inner_hbm, wide * j, wide)
        write(inner, inner_hbm, ff + wide * j, wide)
    for copy in writes:
        copy.wait()


def input_kernel(
    inner_ref, w_in, x_ref, recv_ref, grad_ref, after_ref, pre_ref, packed_ref, inner, normed
):
    del after_ref
    samples, width = x_ref.shape
    wide = 256

    scale = norm_state(x_ref, recv_ref, normed)
    for j in range(inner.shape[1] // samples):
        inner[:, samples * j : samples * j + samples] = inner_ref[samples * j : samples * j + samples, :]
    products = jnp.zeros((samples, 128), F32)
    for d in range(width // wide):
        cols = slice(wide * d, wide * d + wide)
        g = nt(inner[...], w_in[cols, :]) + grad_ref[:, cols].astype(F32)
        pre_ref[:, cols] = g
        p = g * normed[:, cols]
        products = products + p[:, :128] + p[:, 128:]
    mean = jnp.sum(products, axis=1, keepdims=True) / width
    for t in range(width // 128):
        pre_ref[:, tile(t)] = scale * (pre_ref[:, tile(t)] - normed[:, tile(t)] * mean)
    pack(lambda t: pre_ref[:, tile(t)], packed_ref)


def final_kernel(pre_ref, recv_ref, out_ref):
    def write(t, returned):
        out_ref[:, tile(t)] = (pre_ref[:, tile(t)] + returned).astype(BF16)

    unpack(recv_ref, write)


PARTNERS = ((1, 3), (3, 1))
X_FIRST, Z_FIRST = (2, 2, 8, 8), (8, 8, 2, 2)


def grad_kernel(x_first, at, block, own_hbm, other_hbm, right_hbm, right_other_hbm, after_hbm, *refs):
    del after_hbm
    outs_hbm, outs = refs[:2], refs[2:4]
    own, other, right, right_other, in_sem, write_sem = refs[4:]
    rows, columns = outs[0].shape
    wide = 256
    sources = ((own_hbm, at, own), (other_hbm, at, other), (right_hbm, block, right), (right_other_hbm, block, right_other))
    reads, writes = [], []
    for n, (source, begin, target) in enumerate(sources):
        reads.append(pltpu.make_async_copy(source.at[pl.ds(begin, target.shape[0])], target, in_sem.at[n]))
        reads[-1].start()
    for copy in reads:
        copy.wait()
    for k in range(columns // wide):
        cols = slice(wide * k, wide * k + wide)
        g = (nn(own[...], right[cols, :]) + nn(other[...], right_other[cols, :])).astype(BF16)
        if x_first:
            outs[0][:, cols] = g[:rows]
            outs[1][:, cols] = g[rows:]
        else:
            for p in range(16):
                half, to = divmod(4 * (p % 4) + p // 4, 8)
                outs[half][48 * to : 48 * to + 48, cols] = g[48 * p : 48 * p + 48]
        if k % 2 == 1 or k == columns // wide - 1:
            begin = k // 2 * 2
            cols = pl.ds(wide * begin, wide * (k + 1 - begin))
            for n in range(2):
                copy = pltpu.make_async_copy(outs[n].at[:, cols], outs_hbm[n].at[:, cols], write_sem.at[begin + n])
                copy.start()
                writes.append(copy)
    for copy in writes:
        copy.wait()


def params():
    return pltpu.CompilerParams(vmem_limit_bytes=VMEM_LIMIT)


VMEM = pl.BlockSpec(memory_space=pltpu.VMEM)
SMEM = pl.BlockSpec(memory_space=pltpu.SMEM)
ANY = pl.BlockSpec(memory_space=pl.ANY)


def cost(flops, moved):
    return pl.CostEstimate(flops=int(flops), bytes_accessed=int(moved), transcendentals=0)


def shape(dims, dtype=BF16):
    return jax.ShapeDtypeStruct(dims, dtype)


def swap(values):
    return lax.ppermute(values, "dp", [(i, i ^ 1) for i in range(32)])


def gradients(x_first, at, block, columns, own, other, right, right_other, after, name):
    rows, samples = own.shape[0] // 2, own.shape[1]
    piece = shape((rows // 2, columns))
    moved = (2 * rows * samples + 2 * samples * columns + rows * columns) * 2
    return pl.pallas_call(
        functools.partial(grad_kernel, x_first, at, block),
        out_shape=[piece] * 2,
        in_specs=[ANY] * 5,
        out_specs=[ANY] * 2,
        scratch_shapes=[pltpu.VMEM(piece.shape, BF16)] * 2
        + [pltpu.VMEM((rows, samples), BF16)] * 2
        + [pltpu.VMEM((columns, samples), BF16)] * 2
        + [pltpu.SemaphoreType.DMA((4,)), pltpu.SemaphoreType.DMA((columns // 256 + 1,))],
        compiler_params=params(),
        cost_estimate=cost(2 * rows * 2 * samples * columns, moved),
        name=name,
    )(own, other, right, right_other, after)


def reduce_send(scales, step, send):
    return lax.ppermute(send, "dp", [(i, i ^ (PARTNERS[i & 1][step % 2] * scales[step])) for i in range(32)])


def reduce_add(step, keep, got):
    total = keep.astype(F32) + got.astype(F32)
    if step == 3:
        return total.astype(BF16), None
    half = total.shape[0] // 2
    return total[:half].astype(BF16), total[half:].astype(BF16)


def local(block_input, out_cotangent, w_in, w_out):
    samples, _, width = block_input.shape
    ff = w_out.shape[2]
    x = block_input[:, 0]
    cotangent = out_cotangent[:, 0]
    flat_in = w_in[0].reshape(width, 2 * ff)
    weight_out = w_out[0]
    packed_shape = shape((TOK, samples * 3 // 2, 128))
    index = lax.axis_index("dp").astype(jnp.int32).reshape(1)

    packed = pl.pallas_call(
        pack_kernel, out_shape=packed_shape, in_specs=[VMEM], out_specs=VMEM, compiler_params=params(),
        cost_estimate=cost(samples * width, 4 * samples * width), name="pack",
    )(x)
    recv = lax.all_to_all(packed, "token", split_axis=0, concat_axis=0, tiled=True)

    flat = shape((samples, width))
    own, send, inner, out_grad16, held_in = pl.pallas_call(
        main_kernel,
        out_shape=[shape((width, samples)), shape((width + ff, samples)), shape((2 * ff, samples)), flat, pltpu.VMEM((width, 2 * ff), BF16)],
        in_specs=[SMEM, VMEM, VMEM, ANY, ANY, ANY],
        out_specs=[ANY] * 4 + [VMEM],
        scratch_shapes=[
            pltpu.VMEM((width, ff), BF16),
            pltpu.VMEM((samples, width), BF16),
            pltpu.VMEM((samples, width), BF16),
            pltpu.VMEM((samples, width), BF16),
            pltpu.VMEM((samples, ff), BF16),
            pltpu.VMEM((samples, width), F32),
            pltpu.VMEM((samples, ff), F32),
            pltpu.VMEM((samples, ff), F32),
            pltpu.VMEM((width, samples), BF16),
            pltpu.VMEM((width, samples), BF16),
            pltpu.VMEM((width + ff, samples), BF16),
            pltpu.VMEM((2 * ff, samples), BF16),
            pltpu.SemaphoreType.DMA((8,)),
            pltpu.SemaphoreType.DMA,
            pltpu.SemaphoreType.DMA,
            pltpu.SemaphoreType.DMA((14,)),
        ],
        compiler_params=params(),
        cost_estimate=cost(8 * samples * width * ff, 18e6),
        name="main",
    )(index, x, recv, cotangent, flat_in, weight_out)
    other, inner_other = swap(send), swap(inner)

    half, split = width // 2, 768
    down = gradients(True, 0, width, ff, own, other, send, other, inner, "down_grads")
    low = gradients(False, half, 0, split, own, other, inner, inner_other, down[1], "low_grads")
    high = gradients(True, half, split, 2 * ff - split, own, other, inner, inner_other, low[1], "high_grads")
    orders = (X_FIRST, Z_FIRST, X_FIRST)
    kept = [grads[0] for grads in (down, low, high)]
    got = [reduce_send(order, 0, grads[1]) for order, grads in zip(orders, (down, low, high))]

    pre_grad, back = pl.pallas_call(
        input_kernel,
        out_shape=[shape((samples, width), F32), packed_shape],
        in_specs=[VMEM] * 5 + [ANY],
        out_specs=[VMEM] * 2,
        scratch_shapes=[
            pltpu.VMEM((samples, 2 * ff), BF16),
            pltpu.VMEM((samples, width), F32),
        ],
        compiler_params=params(),
        cost_estimate=cost(4 * samples * width * ff, 14e6),
        name="input",
    )(inner, pltpu.with_memory_space_constraint(held_in, pltpu.VMEM), x, recv, out_grad16, high[1])
    returned = lax.all_to_all(back, "token", split_axis=0, concat_axis=0, tiled=True)

    input_grad = pl.pallas_call(
        final_kernel, out_shape=flat, in_specs=[VMEM] * 2, out_specs=VMEM,
        compiler_params=params(), cost_estimate=cost(samples * width, 8 * samples * width), name="final",
    )(pre_grad, returned)

    previous = None
    for which, step in ((0, 0), (1, 0), (2, 0), (0, 1), (2, 1), (1, 1), (2, 2), (0, 2), (1, 2), (0, 3), (1, 3), (2, 3)):
        arrived = got[which]
        if previous is not None:
            arrived, previous = lax.optimization_barrier((arrived, previous))
        if (which, step) == (2, 2):
            arrived, input_grad = lax.optimization_barrier((arrived, input_grad))
        kept[which], sent = reduce_add(step, kept[which], arrived)
        previous = kept[which] if sent is None else sent
        if step < 3:
            got[which] = reduce_send(orders[which], step + 1, sent)

    in_grad = jnp.concatenate(kept[1:], axis=1).reshape(width // 32, 2, ff)
    return (input_grad[:, None, :], in_grad[None], kept[0][None])


def solution(mesh):
    placed = (
        P("dp", "token", None),
        P("dp", "token", None),
        P("token", None, None, None),
        P("token", None, None),
    )
    return jax.shard_map(
        local,
        mesh=mesh,
        in_specs=placed,
        out_specs=(P("dp", "token", None), P("token", "dp", None, None), P("token", "dp", None)),
        check_vma=False,
    )
```

```python
import functools

import jax
import jax.numpy as jnp
from jax import lax
from jax.experimental import pallas as pl
from jax.experimental.pallas import tpu as pltpu
from jax.sharding import PartitionSpec as P

EPS = 1e-06
TOK = 8
F32 = jnp.float32
BF16 = jnp.bfloat16
VMEM_LIMIT = 56 * 1024 * 1024


def low_lanes(rows):
    return lax.broadcasted_iota(jnp.int32, (rows, 128), 1) < 64


def turn(values):
    return pltpu.roll(values, 64, 1)


def pack(read, packed_ref):
    samples = packed_ref.shape[1] * 2 // 3
    half = samples // 2
    low, low_half = low_lanes(samples), low_lanes(half)
    for pair in range(TOK // 2):
        first, middle, last = read(3 * pair), read(3 * pair + 1), read(3 * pair + 2)
        even, odd = packed_ref.at[2 * pair], packed_ref.at[2 * pair + 1]
        even[:samples] = first.astype(BF16)
        even[samples:] = jnp.where(low_half, middle[:half], turn(middle[half:])).astype(BF16)
        odd[:samples] = turn(jnp.where(low, last, middle)).astype(BF16)
        odd[samples:] = jnp.where(low_half, turn(last[:half]), last[half:]).astype(BF16)


def unpack(packed_ref, write):
    samples = packed_ref.shape[1] * 2 // 3
    low = low_lanes(samples)
    for pair in range(TOK // 2):
        even, odd = packed_ref.at[2 * pair], packed_ref.at[2 * pair + 1]
        turned = turn(odd[:samples].astype(F32))
        rest = even[samples:].astype(F32)
        rest = jnp.concatenate([rest, turn(rest)], axis=0)
        rest_odd = odd[samples:].astype(F32)
        rest_odd = jnp.concatenate([turn(rest_odd), rest_odd], axis=0)
        write(3 * pair, even[:samples].astype(F32))
        write(3 * pair + 1, jnp.where(low, rest, turned))
        write(3 * pair + 2, jnp.where(low, turned, rest_odd))


def tile(t):
    return slice(128 * t, 128 * t + 128)


def pack_kernel(x_ref, packed_ref):
    pack(lambda t: x_ref[:, tile(t)].astype(F32), packed_ref)


def nn(a, b):
    return lax.dot_general(a, b, (((1,), (0,)), ((), ())), preferred_element_type=F32)


def nt(a, b):
    return lax.dot_general(a, b, (((1,), (1,)), ((), ())), preferred_element_type=F32)


def norm_state(x_ref, recv_ref, normed_ref):
    samples, width = x_ref.shape
    sums = [jnp.zeros((samples, 128), F32)]

    def add_mixed(t, mixed):
        v = x_ref[:, tile(t)].astype(F32) + mixed
        normed_ref[:, tile(t)] = v
        sums[0] = sums[0] + v * v

    unpack(recv_ref, add_mixed)
    scale = lax.rsqrt(jnp.sum(sums[0], axis=1, keepdims=True) / width + EPS)
    for t in range(width // 128):
        normed_ref[:, tile(t)] = normed_ref[:, tile(t)] * scale
    return scale


def main_kernel(
    index_ref, x_ref, recv_ref, cot_hbm, w_in_hbm, w_out_hbm,
    own_hbm, send_hbm, inner_hbm, grad16_hbm, w_in,
    w_out, cot, state, grad16, hidden, values, slope, silu, turned, own, send, inner,
    in_sem, out_sem, cot_sem, write_sem,
):
    samples, width = x_ref.shape
    ff = w_out.shape[1]
    wide = 256
    steps = ff // wide
    half = width // 2
    writes = []

    def write(source, target, begin, rows):
        place = pl.ds(begin, rows)
        writes.append(pltpu.make_async_copy(source.at[place], target.at[place], write_sem.at[len(writes)]))
        writes[-1].start()

    def w_in_copy(j, c):
        cols = pl.ds(c * ff + j * wide, wide)
        return pltpu.make_async_copy(w_in_hbm.at[:, cols], w_in.at[:, cols], in_sem.at[2 * j + c])

    for j in range(steps):
        w_in_copy(j, 0).start()
        w_in_copy(j, 1).start()
    out_copy = pltpu.make_async_copy(w_out_hbm, w_out, out_sem)
    out_copy.start()
    cot_copy = pltpu.make_async_copy(cot_hbm, cot, cot_sem)
    cot_copy.start()

    rank = index_ref[0]

    def block(place, flavour):
        rx, rz = ((0, 3 - 2 * flavour, 1 + 2 * flavour, 2)[at] for at in divmod(place, 4))
        return 4 * rz + rx

    core = rank & 1

    def spread(at):
        for p in range(16):
            place = slice(at + 48 * p, at + 48 * p + 48)
            mine = (rank ^ (2 * block(p, core))) * 48
            theirs = (rank ^ (2 * block(p, 1 - core) + 1)) * 48
            own[place, :] = turned[pl.ds(pl.multiple_of(mine, 48), 48), :]
            send[place, :] = turned[pl.ds(pl.multiple_of(theirs, 48), 48), :]
        write(send, send_hbm, at, half)
        write(own, own_hbm, at, half)

    norm_state(x_ref, recv_ref, values)
    for t in range(width // 128):
        state[:, tile(t)] = values[:, tile(t)].astype(BF16)

    for j in range(steps):
        cols = slice(wide * j, wide * j + wide)
        w_in_copy(j, 0).wait()
        gate = nn(state[...], w_in[:, cols])
        w_in_copy(j, 1).wait()
        up = nn(state[...], w_in[:, ff + wide * j : ff + wide * j + wide])
        sigma = jax.nn.sigmoid(gate)
        silu_gate = gate * sigma
        part = (silu_gate * up).astype(BF16)
        hidden[:, cols] = part
        send[width + wide * j : width + wide * j + wide, :] = part
        silu[:, cols] = silu_gate
        slope[:, cols] = up * sigma * (1.0 + gate * (1.0 - sigma))
    write(send, send_hbm, width, ff)

    out_copy.wait()
    for d in range(width // wide):
        cols = slice(wide * d, wide * d + wide)
        values[:, cols] = nt(hidden[...], w_out[cols, :]) + state[:, cols].astype(F32)
    for t in range(width // 128):
        turned[tile(t), :] = state[:, tile(t)].T
    spread(half)
    cot_copy.wait()
    squares = jnp.zeros((samples, 128), F32)
    products = jnp.zeros((samples, 128), F32)
    for t in range(width // 128):
        v = values[:, tile(t)]
        squares = squares + v * v
        products = products + v * cot[:, tile(t)].astype(F32)
    scale = lax.rsqrt(jnp.sum(squares, axis=1, keepdims=True) / width + EPS)
    mean = scale * jnp.sum(products, axis=1, keepdims=True) / width
    for t in range(width // 128):
        out_normed = values[:, tile(t)] * scale
        g16 = (scale * (cot[:, tile(t)].astype(F32) - out_normed * mean)).astype(BF16)
        grad16[:, tile(t)] = g16
        turned[tile(t), :] = g16.T
    write(grad16, grad16_hbm, 0, samples)
    spread(0)
    for j in range(steps):
        cols = slice(wide * j, wide * j + wide)
        hidden_grad = nn(grad16[...], w_out[:, cols])
        inner[cols, :] = (hidden_grad * slope[:, cols]).astype(BF16)
        inner[ff + wide * j : ff + wide * j + wide, :] = (hidden_grad * silu[:, cols]).astype(BF16)
        write(inner, inner_hbm, wide * j, wide)
        write(inner, inner_hbm, ff + wide * j, wide)
    for copy in writes:
        copy.wait()


def input_kernel(
    inner_ref, w_in, x_ref, recv_ref, grad_ref, after_ref, pre_ref, packed_ref, inner, normed
):
    del after_ref
    samples, width = x_ref.shape
    wide = 256

    scale = norm_state(x_ref, recv_ref, normed)
    for j in range(inner.shape[1] // samples):
        inner[:, samples * j : samples * j + samples] = inner_ref[samples * j : samples * j + samples, :]
    products = jnp.zeros((samples, 128), F32)
    for d in range(width // wide):
        cols = slice(wide * d, wide * d + wide)
        g = nt(inner[...], w_in[cols, :]) + grad_ref[:, cols].astype(F32)
        pre_ref[:, cols] = g
        p = g * normed[:, cols]
        products = products + p[:, :128] + p[:, 128:]
    mean = jnp.sum(products, axis=1, keepdims=True) / width
    for t in range(width // 128):
        pre_ref[:, tile(t)] = scale * (pre_ref[:, tile(t)] - normed[:, tile(t)] * mean)
    pack(lambda t: pre_ref[:, tile(t)], packed_ref)


def final_kernel(pre_ref, recv_ref, out_ref):
    def write(t, returned):
        out_ref[:, tile(t)] = (pre_ref[:, tile(t)] + returned).astype(BF16)

    unpack(recv_ref, write)


PARTNERS = ((1, 3), (3, 1))
SCALES = (2, 2, 8, 8)


def grad_kernel(at, block, own_hbm, other_hbm, right_hbm, right_other_hbm, after_hbm, *refs):
    del after_hbm
    outs_hbm, outs = refs[:2], refs[2:4]
    own, other, right, right_other, in_sem, write_sem = refs[4:]
    rows, columns = outs[0].shape
    wide = 256
    sources = ((own_hbm, at, own), (other_hbm, at, other), (right_hbm, block, right), (right_other_hbm, block, right_other))
    reads, writes = [], []
    for n, (source, begin, target) in enumerate(sources):
        reads.append(pltpu.make_async_copy(source.at[pl.ds(begin, target.shape[0])], target, in_sem.at[n]))
        reads[-1].start()
    for copy in reads:
        copy.wait()
    for k in range(columns // wide):
        cols = slice(wide * k, wide * k + wide)
        g = (nn(own[...], right[cols, :]) + nn(other[...], right_other[cols, :])).astype(BF16)
        outs[0][:, cols] = g[:rows]
        outs[1][:, cols] = g[rows:]
        if k % 2 == 1:
            cols = pl.ds(wide * (k - 1), 2 * wide)
            for n in range(2):
                copy = pltpu.make_async_copy(outs[n].at[:, cols], outs_hbm[n].at[:, cols], write_sem.at[k - 1 + n])
                copy.start()
                writes.append(copy)
    for copy in writes:
        copy.wait()


def params():
    return pltpu.CompilerParams(vmem_limit_bytes=VMEM_LIMIT)


VMEM = pl.BlockSpec(memory_space=pltpu.VMEM)
SMEM = pl.BlockSpec(memory_space=pltpu.SMEM)
ANY = pl.BlockSpec(memory_space=pl.ANY)


def cost(flops, moved):
    return pl.CostEstimate(flops=int(flops), bytes_accessed=int(moved), transcendentals=0)


def shape(dims, dtype=BF16):
    return jax.ShapeDtypeStruct(dims, dtype)


def swap(values):
    return lax.ppermute(values, "dp", [(i, i ^ 1) for i in range(32)])


def gradients(at, block, columns, own, other, right, right_other, after, name):
    rows, samples = own.shape[0] // 2, own.shape[1]
    piece = shape((rows // 2, columns))
    moved = (2 * rows * samples + 2 * samples * columns + rows * columns) * 2
    return pl.pallas_call(
        functools.partial(grad_kernel, at, block),
        out_shape=[piece] * 2,
        in_specs=[ANY] * 5,
        out_specs=[ANY] * 2,
        scratch_shapes=[pltpu.VMEM(piece.shape, BF16)] * 2
        + [pltpu.VMEM((rows, samples), BF16)] * 2
        + [pltpu.VMEM((columns, samples), BF16)] * 2
        + [pltpu.SemaphoreType.DMA((4,)), pltpu.SemaphoreType.DMA((columns // 256,))],
        compiler_params=params(),
        cost_estimate=cost(2 * rows * 2 * samples * columns, moved),
        name=name,
    )(own, other, right, right_other, after)


def reduce_send(step, send):
    return lax.ppermute(send, "dp", [(i, i ^ (PARTNERS[i & 1][step % 2] * SCALES[step])) for i in range(32)])


def reduce_add(step, keep, got):
    total = keep.astype(F32) + got.astype(F32)
    if step == 3:
        return total.astype(BF16), None
    half = total.shape[0] // 2
    return total[:half].astype(BF16), total[half:].astype(BF16)


def local(block_input, out_cotangent, w_in, w_out):
    samples, _, width = block_input.shape
    ff = w_out.shape[2]
    x = block_input[:, 0]
    cotangent = out_cotangent[:, 0]
    flat_in = w_in[0].reshape(width, 2 * ff)
    weight_out = w_out[0]
    packed_shape = shape((TOK, samples * 3 // 2, 128))
    index = lax.axis_index("dp").astype(jnp.int32).reshape(1)

    packed = pl.pallas_call(
        pack_kernel, out_shape=packed_shape, in_specs=[VMEM], out_specs=VMEM, compiler_params=params(),
        cost_estimate=cost(samples * width, 4 * samples * width), name="pack",
    )(x)
    recv = lax.all_to_all(packed, "token", split_axis=0, concat_axis=0, tiled=True)

    flat = shape((samples, width))
    own, send, inner, out_grad16, held_in = pl.pallas_call(
        main_kernel,
        out_shape=[shape((width, samples)), shape((width + ff, samples)), shape((2 * ff, samples)), flat, pltpu.VMEM((width, 2 * ff), BF16)],
        in_specs=[SMEM, VMEM, VMEM, ANY, ANY, ANY],
        out_specs=[ANY] * 4 + [VMEM],
        scratch_shapes=[
            pltpu.VMEM((width, ff), BF16),
            pltpu.VMEM((samples, width), BF16),
            pltpu.VMEM((samples, width), BF16),
            pltpu.VMEM((samples, width), BF16),
            pltpu.VMEM((samples, ff), BF16),
            pltpu.VMEM((samples, width), F32),
            pltpu.VMEM((samples, ff), F32),
            pltpu.VMEM((samples, ff), F32),
            pltpu.VMEM((width, samples), BF16),
            pltpu.VMEM((width, samples), BF16),
            pltpu.VMEM((width + ff, samples), BF16),
            pltpu.VMEM((2 * ff, samples), BF16),
            pltpu.SemaphoreType.DMA((8,)),
            pltpu.SemaphoreType.DMA,
            pltpu.SemaphoreType.DMA,
            pltpu.SemaphoreType.DMA((14,)),
        ],
        compiler_params=params(),
        cost_estimate=cost(8 * samples * width * ff, 18e6),
        name="main",
    )(index, x, recv, cotangent, flat_in, weight_out)
    other, inner_other = swap(send), swap(inner)

    half = width // 2
    down = gradients(0, width, ff, own, other, send, other, inner, "down_grads")
    gate = gradients(half, 0, ff, own, other, inner, inner_other, down[1], "gate_grads")
    up = gradients(half, ff, ff, own, other, inner, inner_other, gate[1], "up_grads")
    kept = [grads[0] for grads in (down, gate, up)]
    got = [reduce_send(0, grads[1]) for grads in (down, gate, up)]

    pre_grad, back = pl.pallas_call(
        input_kernel,
        out_shape=[shape((samples, width), F32), packed_shape],
        in_specs=[VMEM] * 5 + [ANY],
        out_specs=[VMEM] * 2,
        scratch_shapes=[
            pltpu.VMEM((samples, 2 * ff), BF16),
            pltpu.VMEM((samples, width), F32),
        ],
        compiler_params=params(),
        cost_estimate=cost(4 * samples * width * ff, 14e6),
        name="input",
    )(inner, pltpu.with_memory_space_constraint(held_in, pltpu.VMEM), x, recv, out_grad16, up[1])
    returned = lax.all_to_all(back, "token", split_axis=0, concat_axis=0, tiled=True)

    input_grad = pl.pallas_call(
        final_kernel, out_shape=flat, in_specs=[VMEM] * 2, out_specs=VMEM,
        compiler_params=params(), cost_estimate=cost(samples * width, 8 * samples * width), name="final",
    )(pre_grad, returned)

    previous = None
    for which, step in ((0, 0), (1, 0), (0, 1), (2, 0), (1, 1), (2, 1), (0, 2), (1, 2), (2, 2), (0, 3), (1, 3), (2, 3)):
        arrived = got[which]
        if previous is not None:
            arrived, previous = lax.optimization_barrier((arrived, previous))
        if (which, step) == (2, 2):
            arrived, input_grad = lax.optimization_barrier((arrived, input_grad))
        kept[which], sent = reduce_add(step, kept[which], arrived)
        previous = kept[which] if sent is None else sent
        if step < 3:
            got[which] = reduce_send(step + 1, sent)

    return (input_grad[:, None, :], jnp.stack(kept[1:], axis=1)[None], kept[0][None])


def solution(mesh):
    placed = (
        P("dp", "token", None),
        P("dp", "token", None),
        P("token", None, None, None),
        P("token", None, None),
    )
    return jax.shard_map(
        local,
        mesh=mesh,
        in_specs=placed,
        out_specs=(P("dp", "token", None), P("token", "dp", None, None), P("token", "dp", None)),
        check_vma=False,
    )
```
